128 devices in a mesh: seq: 16 (over x_lo, y, core), col: 8 (over z, x_hi).
Axes of the slice: x: 4 (x_hi: 2, x_lo: 2; x = x_hi * 2 + x_lo), y: 4, z: 4, core: 2. Of those that a mesh axis runs over, the one named last changes fastest.
Arguments:
- aligned_sequence_embeddings: bfloat16 [64, 1024, 768], P('seq', 'col'), may hold values from -6 to 6
- horizontal_scaling_factor: float32 [768], replicated, may hold values from 0.1 to 1.9
- horizontal_attend_matrices: bfloat16 [768, 2304], replicated, may hold values from -0.36084392 to 0.36084392
- horizontal_exit_matrix: bfloat16 [768, 768], replicated, may hold values from -0.21875 to 0.21875
- vertical_scaling_factor: float32 [768], replicated, may hold values from 0.1 to 1.9
- vertical_attend_matrices: bfloat16 [768, 2304], replicated, may hold values from -2.598076 to 2.598076
- vertical_exit_matrix: bfloat16 [768, 768], replicated, may hold values from -0.21875 to 0.21875
- dense_scaling_factor: float32 [768], replicated, may hold values from 0.1 to 1.9
- dense_expand_matrix: bfloat16 [768, 3072], replicated, may hold values from -0.21875 to 0.21875
- dense_shrink_matrix: bfloat16 [3072, 768], replicated, may hold values from -0.109375 to 0.109375
Outputs:
- layer_out: bfloat16 [64, 1024, 768], P('seq', 'col')
The draws below stay inside these ranges and needn't reach their ends.
All inputs are finite; a program needn't handle non-finite values.
Results may differ from the reference program's by a relative error of at most 0.013.
Values may be sent and summed in bfloat16 or wider, within the bound.
No kernel may reach another device: no remote copies, remote signals or barrier semaphores. Data moves between devices by JAX's collectives and lax.ppermute only.
A program may use at most 128 MiB of HBM per device.

```python
import math
import jax
import jax.numpy as jnp
from jax import lax

D = 768
HEADS = 12
FF = 3072
ROWS = 64
COLS = 1024


def drawn_weights(key):
    draws = jax.random.truncated_normal(key, -6.0, 6.0, (D, 3 * D), jnp.float32)
    return draws * (1.0 / math.sqrt(D))


def draw_aligned_sequence_embeddings(key, part):
    key = jax.random.fold_in(key, 5)
    return jax.random.truncated_normal(key, -6.0, 6.0, (ROWS, COLS, D), jnp.float32).astype(jnp.bfloat16)


def draw_horizontal_attend_matrices(key, part):
    key = jax.random.fold_in(key, 11)
    return drawn_weights(key).astype(jnp.bfloat16)


def draw_vertical_attend_matrices(key, part):
    key = jax.random.fold_in(key, 17)
    return drawn_weights(key).astype(jnp.bfloat16)


def normal_values(stream_key, shape, spread, reach, held_as=jnp.bfloat16):
    drawn = spread * jax.random.normal(stream_key, shape, jnp.float32)
    return jnp.clip(drawn, min=-reach, max=reach).astype(held_as)


def setup_inputs(seed: int = 0) -> dict:
    streams_of = jax.random.split(jax.random.key(seed), 11)
    aligned_sequence_embeddings = draw_aligned_sequence_embeddings(jax.random.fold_in(streams_of[10], 71), 0)
    horizontal_scaling_factor = jnp.clip(1.0 + 0.18 * jax.random.normal(streams_of[1], (D,), jnp.float32), 0.1, 1.9)
    horizontal_attend_matrices = draw_horizontal_attend_matrices(jax.random.fold_in(streams_of[10], 71), 0)
    horizontal_exit_matrix = normal_values(streams_of[3], (D, D), D ** -0.5, 0.21875)
    vertical_scaling_factor = jnp.clip(1.0 + 0.18 * jax.random.normal(streams_of[4], (D,), jnp.float32), 0.1, 1.9)
    vertical_attend_matrices = draw_vertical_attend_matrices(jax.random.fold_in(streams_of[10], 71), 0)
    vertical_exit_matrix = normal_values(streams_of[6], (D, D), D ** -0.5, 0.21875)
    dense_scaling_factor = jnp.clip(1.0 + 0.18 * jax.random.normal(streams_of[7], (D,), jnp.float32), 0.1, 1.9)
    dense_expand_matrix = normal_values(streams_of[8], (D, FF), D ** -0.5, 0.21875)
    dense_shrink_matrix = normal_values(streams_of[9], (FF, D), FF ** -0.5, 0.109375)
    return {"aligned_sequence_embeddings": aligned_sequence_embeddings, "horizontal_scaling_factor": horizontal_scaling_factor, "horizontal_attend_matrices": horizontal_attend_matrices, "horizontal_exit_matrix": horizontal_exit_matrix, "vertical_scaling_factor": vertical_scaling_factor, "vertical_attend_matrices": vertical_attend_matrices, "vertical_exit_matrix": vertical_exit_matrix, "dense_scaling_factor": dense_scaling_factor, "dense_expand_matrix": dense_expand_matrix, "dense_shrink_matrix": dense_shrink_matrix}


def normalize(stream, gain):
    mean = lax.optimization_barrier(jnp.mean(stream, axis=-1, keepdims=True))
    centred = stream - mean
    var = lax.optimization_barrier(jnp.mean(centred * centred, axis=-1, keepdims=True))
    return (centred * lax.rsqrt(var + 1e-05) * gain).astype(jnp.bfloat16)

def project(normed, weight):
    horizontal_extent, vertical_extent, embedding_breadth = normed.shape
    flat = jnp.dot(normed.reshape(horizontal_extent * vertical_extent, embedding_breadth), weight, preferred_element_type=jnp.float32)
    return flat.reshape(horizontal_extent, vertical_extent, weight.shape[1])

def softmax_last(scores):
    top = lax.optimization_barrier(jnp.max(scores, axis=-1, keepdims=True))
    expo = jnp.exp(scores - top)
    return expo / lax.optimization_barrier(jnp.sum(expo, axis=-1, keepdims=True))

def reference(aligned_sequence_embeddings, horizontal_scaling_factor, horizontal_attend_matrices, horizontal_exit_matrix, vertical_scaling_factor, vertical_attend_matrices, vertical_exit_matrix, dense_scaling_factor, dense_expand_matrix, dense_shrink_matrix):
    global_sequence_number, global_position_number, embedding_breadth = aligned_sequence_embeddings.shape
    head_dim = embedding_breadth // HEADS
    skip_connection0 = aligned_sequence_embeddings.astype(jnp.float32)
    row_proj = project(normalize(skip_connection0, horizontal_scaling_factor), horizontal_attend_matrices).astype(jnp.bfloat16)
    query, keys, values = jnp.split(row_proj, 3, axis=-1)

    def by_head(array):
        return array.reshape(global_sequence_number, global_position_number, HEADS, head_dim).transpose(2, 0, 1, 3)
    scale = head_dim ** (-0.5) / math.sqrt(global_sequence_number)

    def one_head(operands):
        q_head, k_head, v_head = operands
        tied = jnp.einsum('rie,rje->ij', q_head.astype(jnp.float32), k_head.astype(jnp.float32)) * scale
        weights = softmax_last(tied).astype(jnp.bfloat16)
        mixed = jnp.einsum('ij,rje->rie', weights.astype(jnp.float32), v_head.astype(jnp.float32))
        return mixed.astype(jnp.bfloat16)
    row_mix = lax.map(one_head, (by_head(query), by_head(keys), by_head(values)))
    row_mix = row_mix.transpose(1, 2, 0, 3).reshape(global_sequence_number, global_position_number, embedding_breadth)
    stream1 = skip_connection0 + project(row_mix, horizontal_exit_matrix)
    col_proj = project(normalize(stream1, vertical_scaling_factor), vertical_attend_matrices).astype(jnp.bfloat16)
    cq, ck, cv = jnp.split(col_proj, 3, axis=-1)
    cq = cq.reshape(global_sequence_number, global_position_number, HEADS, head_dim).astype(jnp.float32)
    ck = ck.reshape(global_sequence_number, global_position_number, HEADS, head_dim).astype(jnp.float32)
    cv = cv.reshape(global_sequence_number, global_position_number, HEADS, head_dim).astype(jnp.float32)
    col_scores = jnp.einsum('rche,sche->chrs', cq, ck) * head_dim ** (-0.5)
    col_weights = softmax_last(col_scores).astype(jnp.bfloat16)
    col_mix = jnp.einsum('chrs,sche->rche', col_weights.astype(jnp.float32), cv).astype(jnp.bfloat16)
    stream2 = stream1 + project(col_mix.reshape(global_sequence_number, global_position_number, embedding_breadth), vertical_exit_matrix)
    hidden = jax.nn.gelu(project(normalize(stream2, dense_scaling_factor), dense_expand_matrix), approximate=False).astype(jnp.bfloat16)
    return (stream2 + project(hidden, dense_shrink_matrix)).astype(jnp.bfloat16)
```

```python
import math

import jax
import jax.numpy as jnp
from jax import lax
from jax.experimental import pallas as pl
from jax.experimental.pallas import tpu as pltpu
from jax.sharding import PartitionSpec as P

AXES = ("seq", "col")
HEADS = 12
E = 64
BF = jnp.bfloat16
F32 = jnp.float32
VMEM_LIMIT = 56 * 1024 * 1024


def device(xl, y, c, z, xh):
    return ((xl * 4 + y) * 2 + c) * 8 + z * 2 + xh


R2, R4 = range(2), range(4)
X_RINGS = [[device(xl, y, c, z, xh) for xh in R2 for xl in R2] for y in R4 for c in R2 for z in R4]
Y_RINGS = [[device(xl, y, c, z, xh) for y in R4] for xl in R2 for c in R2 for z in R4 for xh in R2]
Z_RINGS = [[device(xl, y, c, z, xh) for z in R4] for xl in R2 for y in R4 for c in R2 for xh in R2]
PLANES = [[device(xl, y, c, z, xh) for xh in R2 for xl in R2 for y in R4] for c in R2 for z in R4]
OTHER_CORE = [
    (device(xl, y, c, z, xh), device(xl, y, 1 - c, z, xh))
    for xl in R2 for y in R4 for c in R2 for z in R4 for xh in R2
]


def params():
    return pltpu.CompilerParams(vmem_limit_bytes=VMEM_LIMIT)


def swap(array, groups):
    return lax.all_to_all(array, AXES, split_axis=0, concat_axis=0, tiled=True, axis_index_groups=groups)


def gather(array, groups):
    return lax.all_gather(array, AXES, axis=0, tiled=False, axis_index_groups=groups)


def to_other_core(array):
    return lax.ppermute(array, AXES, OTHER_CORE)


def mm(a, b):
    return jnp.dot(a, b, preferred_element_type=F32)


def mm_t(a, b):
    return lax.dot_general(a, b, (((1,), (1,)), ((), ())), preferred_element_type=F32)


def normalize(stream, gain):
    mean = jnp.mean(stream, axis=-1, keepdims=True)
    centred = stream - mean
    var = jnp.mean(centred * centred, axis=-1, keepdims=True)
    return (centred * lax.rsqrt(var + 1e-05) * gain).astype(BF)


def write_pairs(normed, weight, out):
    low = lax.broadcasted_iota(jnp.int32, (128, 128), 1) < E
    for rp in range(2):
        first = mm(normed[2 * rp * 128 : (2 * rp + 1) * 128, :], weight)
        second = mm(normed[(2 * rp + 1) * 128 : (2 * rp + 2) * 128, :], weight)
        for t in range(6):
            a, b = first[:, t * 128 : (t + 1) * 128], second[:, t * 128 : (t + 1) * 128]
            pair = (
                jnp.where(low, a, pltpu.roll(b, E, 1)),
                jnp.where(low, pltpu.roll(a, E, 1), b),
            )
            for k in range(2):
                g, h = (2 * t + k) // 3, (2 * t + k) % 3
                out[g, rp, :, h * 128 : (h + 1) * 128] = pair[k].astype(BF)


def key_kernel(x_ref, gain_ref, w_ref, normed_ref, out_ref):
    normed_ref[...] = normalize(x_ref[...].astype(F32), gain_ref[...])
    write_pairs(normed_ref[...], w_ref[...], out_ref)


def key_proj(x, gain, weight):
    return pl.pallas_call(
        key_kernel,
        grid=(1,),
        in_specs=[
            pl.BlockSpec((512, 768), lambda i: (0, 0)),
            pl.BlockSpec((1, 768), lambda i: (0, 0)),
            pl.BlockSpec((768, 768), lambda i: (0, 1)),
        ],
        out_specs=[
            pl.BlockSpec((512, 768), lambda i: (0, 0)),
            pl.BlockSpec((4, 2, 128, 384), lambda i: (0, 0, 0, 0)),
        ],
        out_shape=[
            jax.ShapeDtypeStruct((512, 768), BF),
            jax.ShapeDtypeStruct((4, 2, 128, 384), BF),
        ],
        compiler_params=params(),
        name="key_proj",
    )(x, gain, weight)


def query_value_kernel(normed_ref, w_ref, out_ref):
    write_pairs(normed_ref[...], w_ref[...], out_ref.at[:, 0])


def query_value_proj(normed, weight):
    return pl.pallas_call(
        query_value_kernel,
        grid=(2,),
        in_specs=[
            pl.BlockSpec((512, 768), lambda i: (0, 0)),
            pl.BlockSpec((768, 768), lambda i: (0, 2 * i)),
        ],
        out_specs=pl.BlockSpec((4, 1, 2, 128, 384), lambda i: (0, i, 0, 0, 0)),
        out_shape=jax.ShapeDtypeStruct((4, 2, 2, 128, 384), BF),
        compiler_params=params(),
        name="query_value_proj",
    )(normed, weight)


def scores_kernel(q0_ref, q1_ref, k0_ref, k1_ref, out_ref):
    def query(xh):
        return jnp.concatenate(
            [q[xh * 2 + xl, rp] for q in (q0_ref, q1_ref) for xl in range(2) for rp in range(2)], axis=1
        )

    def keys(z, xh):
        return jnp.concatenate(
            [k[z, xh * 2 + xl, rp] for k in (k0_ref, k1_ref) for xl in range(2) for rp in range(2)], axis=1
        )

    left = jnp.concatenate([query(0), query(1)], axis=0)
    for z in range(4):
        right = jnp.concatenate([keys(z, 0), keys(z, 1)], axis=0)
        out_ref[:, 0, :, z * 256 : (z + 1) * 256] = mm_t(left, right).reshape(4, 32, 256)


def partial_scores(q0, q1, k0, k1):
    q_spec = pl.BlockSpec((4, 2, 64, 128), lambda h: (0, 0, 0, h))
    k_spec = pl.BlockSpec((4, 4, 2, 128, 128), lambda h: (0, 0, 0, 0, h))
    return pl.pallas_call(
        scores_kernel,
        grid=(3,),
        in_specs=[q_spec, q_spec, k_spec, k_spec],
        out_specs=pl.BlockSpec((4, 1, 32, 1024), lambda h: (0, h, 0, 0)),
        out_shape=jax.ShapeDtypeStruct((4, 3, 32, 1024), F32),
        compiler_params=params(),
        name="partial_scores",
    )(q0, q1, k0, k1)


def softmax_kernel(scale, parts_ref, out_ref):
    tied = (parts_ref[0] + parts_ref[1] + parts_ref[2] + parts_ref[3]) * scale
    expo = jnp.exp(tied - jnp.max(tied, axis=-1, keepdims=True))
    out_ref[...] = (expo / jnp.sum(expo, axis=-1, keepdims=True)).astype(BF)


def row_softmax(parts, scale):
    return pl.pallas_call(
        lambda *refs: softmax_kernel(scale, *refs),
        grid=(3,),
        in_specs=[pl.BlockSpec((4, 1, 32, 1024), lambda h: (0, h, 0, 0))],
        out_specs=pl.BlockSpec((1, 32, 1024), lambda h: (h, 0, 0)),
        out_shape=jax.ShapeDtypeStruct((3, 32, 1024), BF),
        compiler_params=params(),
        name="row_softmax",
    )(parts)


def mix_kernel(core_ref, w_ref, v0_ref, v1_ref, out_ref):
    weights = w_ref[:, 0].reshape(128, 1024)
    for k, v in enumerate((v0_ref, v1_ref)):
        owner = (core_ref[0] + k) % 2
        for xl in range(2):
            right = jnp.concatenate(
                [
                    jnp.concatenate([v[z, xh * 2 + xl, 0], v[z, xh * 2 + xl, 1]], axis=1)
                    for z in range(4)
                    for xh in range(2)
                ],
                axis=0,
            )
            mixed = mm(weights, right)
            pair = jnp.concatenate(
                [mixed[:, :128].reshape(16, 8, 128), mixed[:, 128:].reshape(16, 8, 128)], axis=1
            )
            out_ref[:, pl.ds(owner, 1), xl * 16 : (xl + 1) * 16, :] = pair.astype(BF)[:, None]


def row_mix(core, weights, v0, v1):
    v_spec = pl.BlockSpec((4, 4, 2, 128, 128), lambda h: (0, 0, 0, 0, h))
    return pl.pallas_call(
        mix_kernel,
        grid=(3,),
        in_specs=[
            pl.BlockSpec(memory_space=pltpu.SMEM),
            pl.BlockSpec((4, 1, 32, 1024), lambda h: (0, h, 0, 0)),
            v_spec,
            v_spec,
        ],
        out_specs=pl.BlockSpec((16, 2, 32, 128), lambda h: (0, 0, 0, h)),
        out_shape=jax.ShapeDtypeStruct((16, 2, 32, 384), BF),
        compiler_params=params(),
        name="row_mix",
    )(core, weights, v0, v1)


def column_kernel(
    mix_ref, x_ref, gain_col_ref, gain_ffn_ref, exit_row_hbm, attend_hbm, exit_col_hbm, expand_hbm, shrink_hbm,
    out_ref, exit_row, attend, exit_col, expand, shrink, qkv, stream, col_mix, sems,
):
    copies = [
        pltpu.make_async_copy(src, dst, sems.at[i])
        for i, (src, dst) in enumerate(
            [
                (exit_row_hbm, exit_row),
                (attend_hbm, attend),
                (exit_col_hbm, exit_col),
                (expand_hbm, expand),
                (shrink_hbm, shrink),
            ]
        )
    ]
    for copy in copies:
        copy.start()

    low = lax.broadcasted_iota(jnp.int32, (64, 128), 1) < E
    halves = ([], [])
    for y in range(4):
        tiles = ([], [])
        for t in range(6):
            (g0, h0), (g1, h1) = divmod(2 * t, 3), divmod(2 * t + 1, 3)
            a = mix_ref[g0 * 4 + y, :, h0 * 128 : (h0 + 1) * 128].astype(F32)
            b = mix_ref[g1 * 4 + y, :, h1 * 128 : (h1 + 1) * 128].astype(F32)
            tiles[0].append(jnp.where(low, a, pltpu.roll(b, E, 1)).astype(BF))
            tiles[1].append(jnp.where(low, pltpu.roll(a, E, 1), b).astype(BF))
        for k in range(2):
            halves[k].append(jnp.concatenate(tiles[k], axis=1))
    copies[0].wait()
    exits = [mm(jnp.concatenate(halves[k], axis=0), exit_row[...]).reshape(32, 1, 8, 768) for k in range(2)]
    exits = jnp.concatenate(exits, axis=1).reshape(512, 768)
    x = jnp.concatenate([x_ref[(xl * 4 + y) * 2 + c] for y in range(4) for c in range(2) for xl in range(2)], axis=0)
    stream[...] = x.astype(F32) + exits

    place = lax.broadcasted_iota(jnp.int32, (512, 512), 0)
    token = lax.broadcasted_iota(jnp.int32, (512, 512), 1)
    by_column = ((place % 64) * 8 + place // 64 == token).astype(F32).astype(BF)
    by_token = ((token % 64) * 8 + token // 64 == place).astype(F32).astype(BF)
    normed = mm(by_column, normalize(stream[...], gain_col_ref[...])).astype(BF)
    copies[1].wait()
    qkv[...] = mm(normed, attend[...]).astype(BF)
    group = lax.broadcasted_iota(jnp.int32, (256, 256), 0) // E == lax.broadcasted_iota(jnp.int32, (256, 256), 1) // E
    group = group.astype(F32).astype(BF)
    segment = lax.broadcasted_iota(jnp.int32, (64, 128), 1) < E
    for c in range(8):
        for g in range(3):
            rows, lanes = slice(c * 64, (c + 1) * 64), g * 256
            q = qkv[rows, lanes : lanes + 256]
            k = qkv[rows, 768 + lanes : 768 + lanes + 256]
            v = qkv[rows, 1536 + lanes : 1536 + lanes + 256]
            k = jnp.concatenate([k] * 4, axis=0) * group
            v = jnp.concatenate([v] * 4, axis=0) * group
            scores = mm_t(q, k) * (E ** -0.5)
            weights = []
            for half in range(2):
                s = scores[:, half * 128 : (half + 1) * 128]
                top0 = jnp.max(jnp.where(segment, s, -jnp.inf), axis=-1, keepdims=True)
                top1 = jnp.max(jnp.where(segment, -jnp.inf, s), axis=-1, keepdims=True)
                expo = jnp.exp(s - jnp.where(segment, top0, top1))
                sum0 = jnp.sum(jnp.where(segment, expo, 0.0), axis=-1, keepdims=True)
                sum1 = jnp.sum(jnp.where(segment, 0.0, expo), axis=-1, keepdims=True)
                weights.append((expo / jnp.where(segment, sum0, sum1)).astype(BF))
            col_mix[rows, lanes : lanes + 256] = mm(jnp.concatenate(weights, axis=1), v).astype(BF)
    mixed = mm(by_token, col_mix[...]).astype(BF)
    copies[2].wait()
    stream[...] += mm(mixed, exit_col[...])

    normed = normalize(stream[...], gain_ffn_ref[...])
    copies[3].wait()
    copies[4].wait()
    for f in range(6):
        cols = slice(f * 512, (f + 1) * 512)
        pre = mm(normed, expand[:, cols])
        hidden = (0.5 * pre * (1.0 + lax.erf(pre * math.sqrt(0.5)))).astype(BF)
        stream[...] += mm(hidden, shrink[cols, :])
    done = stream[...].astype(BF)
    for i, (y, c, xl) in enumerate((y, c, xl) for y in range(4) for c in range(2) for xl in range(2)):
        out_ref[(xl * 4 + y) * 2 + c] = done[i * 32 : (i + 1) * 32, :]


def column_part(mix, x, gain_col, gain_ffn, exit_row, attend, exit_col, expand, shrink):
    whole = pl.BlockSpec(memory_space=pltpu.VMEM)
    hbm = pl.BlockSpec(memory_space=pl.ANY)
    return pl.pallas_call(
        column_kernel,
        in_specs=[whole] * 4 + [hbm] * 5,
        out_specs=whole,
        out_shape=jax.ShapeDtypeStruct((16, 32, 768), BF),
        scratch_shapes=[pltpu.VMEM(w.shape, BF) for w in (exit_row, attend, exit_col, expand, shrink)]
        + [
            pltpu.VMEM((512, 2304), BF),
            pltpu.VMEM((512, 768), F32),
            pltpu.VMEM((512, 768), BF),
            pltpu.SemaphoreType.DMA((5,)),
        ],
        compiler_params=params(),
        name="column_part",
    )(mix, x, gain_col, gain_ffn, exit_row, attend, exit_col, expand, shrink)


def local(
    embeddings,
    gain_row,
    attend_row,
    exit_row,
    gain_col,
    attend_col,
    exit_col,
    gain_ffn,
    expand,
    shrink,
):
    core = lax.axis_index("seq") % 2
    scale = E ** (-0.5) / math.sqrt(embeddings.shape[0] * lax.axis_size("seq"))

    normed, keys = key_proj(embeddings.reshape(512, 768), gain_row.reshape(1, 768), attend_row)
    keys = swap(keys, X_RINGS)
    keys0 = gather(keys, Z_RINGS)
    queries_values = swap(query_value_proj(normed, attend_row), X_RINGS)
    queries, values = queries_values[:, 0], queries_values[:, 1]
    queries0 = lax.dynamic_slice_in_dim(queries, core * 64, 64, axis=2)
    queries1 = to_other_core(lax.dynamic_slice_in_dim(queries, (1 - core) * 64, 64, axis=2))
    values0 = gather(values, Z_RINGS)

    x = embeddings.reshape(4, 2, 8, 8, 768).transpose(2, 1, 0, 3, 4).reshape(16, 32, 768)
    x = lax.all_to_all(x, "seq", split_axis=0, concat_axis=0, tiled=True)

    keys1 = to_other_core(keys0)
    parts = swap(partial_scores(queries0, queries1, keys0, keys1), Y_RINGS)
    weights = row_softmax(parts, scale)
    weights = swap(jnp.broadcast_to(weights[None], (4, 3, 32, 1024)), Y_RINGS)
    values1 = to_other_core(values0)
    mix = row_mix(core.reshape(1).astype(jnp.int32), weights, values0, values1)
    mix = swap(mix, PLANES).reshape(16, 64, 384)

    out = column_part(
        mix, x, gain_col.reshape(1, 768), gain_ffn.reshape(1, 768), exit_row, attend_col, exit_col, expand, shrink
    )
    out = lax.all_to_all(out, "seq", split_axis=0, concat_axis=0, tiled=True)
    return out.reshape(8, 2, 4, 8, 768).transpose(2, 1, 0, 3, 4).reshape(4, 128, 768)


def solution(mesh):
    in_specs = (P("seq", "col", None), P(), P(), P(), P(), P(), P(), P(), P(), P())
    out_specs = P("seq", "col", None)
    return jax.shard_map(local, mesh=mesh, in_specs=in_specs, out_specs=out_specs, check_vma=False)
```

```python
import math

import jax
import jax.numpy as jnp
from jax import lax
from jax.experimental import pallas as pl
from jax.experimental.pallas import tpu as pltpu
from jax.sharding import PartitionSpec as P

AXES = ("seq", "col")
HEADS = 12
E = 64
BF = jnp.bfloat16
F32 = jnp.float32
VMEM_LIMIT = 56 * 1024 * 1024


def device(xl, y, c, z, xh):
    return ((xl * 4 + y) * 2 + c) * 8 + z * 2 + xh


R2, R4 = range(2), range(4)
Y_RINGS = [[device(xl, y, c, z, xh) for y in R4] for xl in R2 for c in R2 for z in R4 for xh in R2]
Z_RINGS = [[device(xl, y, c, z, xh) for z in R4] for xl in R2 for y in R4 for c in R2 for xh in R2]
PLANES = [[device(xl, y, c, z, xh) for xh in R2 for xl in R2 for y in R4] for c in R2 for z in R4]


def shifts(dx=0, dy=0, dz=0, dc=0):
    pairs = []
    for x in R4:
        for y in R4:
            for c in R2:
                for z in R4:
                    to = ((x + dx) % 4, (y + dy) % 4, (c + dc) % 2, (z + dz) % 4)
                    pairs.append((device(x % 2, y, c, z, x // 2), device(to[0] % 2, *to[1:], to[0] // 2)))
    return pairs


def params():
    return pltpu.CompilerParams(vmem_limit_bytes=VMEM_LIMIT)


def swap(array, groups):
    return lax.all_to_all(array, AXES, split_axis=0, concat_axis=0, tiled=True, axis_index_groups=groups)


def gather(array, groups):
    return lax.all_gather(array, AXES, axis=0, tiled=False, axis_index_groups=groups)


def send(array, **by):
    return lax.ppermute(array, AXES, shifts(**by))


def to_other_core(array):
    return send(array, dc=1)


def mm(a, b):
    return jnp.dot(a, b, preferred_element_type=F32)


def mm_t(a, b):
    return lax.dot_general(a, b, (((1,), (1,)), ((), ())), preferred_element_type=F32)


def normalize(stream, gain):
    mean = jnp.mean(stream, axis=-1, keepdims=True)
    centred = stream - mean
    var = jnp.mean(centred * centred, axis=-1, keepdims=True)
    return (centred * lax.rsqrt(var + 1e-05) * gain).astype(BF)


CORE, X, Y, Z = range(4)
SCALARS = pl.BlockSpec(memory_space=pltpu.SMEM)


def write_pieces(place_ref, normed, weight, pieces, outs):
    low = lax.broadcasted_iota(jnp.int32, (128, 128), 1) < E
    for rp in range(2):
        first = mm(normed[2 * rp * 128 : (2 * rp + 1) * 128, :], weight)
        second = mm(normed[(2 * rp + 1) * 128 : (2 * rp + 2) * 128, :], weight)
        for t in range(6):
            a, b = first[:, t * 128 : (t + 1) * 128], second[:, t * 128 : (t + 1) * 128]
            pair = (
                jnp.where(low, a, pltpu.roll(b, E, 1)),
                jnp.where(low, pltpu.roll(a, E, 1), b),
            )
            for k in range(2):
                g, h = (2 * t + k) // 3, (2 * t + k) % 3
                pieces[g, rp, :, h * 128 : (h + 1) * 128] = pair[k].astype(BF)
    for s, out in enumerate(outs):
        out[...] = pieces[(place_ref[X] + s) % 4].reshape(out.shape)


def key_kernel(place_ref, x_ref, gain_ref, w_ref, normed_ref, *refs):
    normed_ref[...] = normalize(x_ref[...].astype(F32), gain_ref[...][None, :])
    write_pieces(place_ref, normed_ref[...], w_ref[...], refs[4], refs[:4])


def key_proj(place, x, gain, weight):
    piece = (2, 128, 384)
    return pl.pallas_call(
        key_kernel,
        grid=(1,),
        in_specs=[
            SCALARS,
            pl.BlockSpec((512, 768), lambda i: (0, 0)),
            pl.BlockSpec((768,), lambda i: (0,)),
            pl.BlockSpec((768, 768), lambda i: (0, 1)),
        ],
        out_specs=[pl.BlockSpec((512, 768), lambda i: (0, 0))] + [pl.BlockSpec(piece, lambda i: (0, 0, 0))] * 4,
        out_shape=[jax.ShapeDtypeStruct((512, 768), BF)] + [jax.ShapeDtypeStruct(piece, BF)] * 4,
        scratch_shapes=[pltpu.VMEM((4,) + piece, BF)],
        compiler_params=params(),
        name="key_proj",
    )(place, x, gain, weight)


def query_value_kernel(place_ref, normed_ref, w_ref, *refs):
    write_pieces(place_ref, normed_ref[...], w_ref[...], refs[4], refs[:4])


def query_value_proj(place, normed, weight):
    piece = (1, 2, 128, 384)
    return pl.pallas_call(
        query_value_kernel,
        grid=(2,),
        in_specs=[
            SCALARS,
            pl.BlockSpec((512, 768), lambda i: (0, 0)),
            pl.BlockSpec((768, 768), lambda i: (0, 2 * i)),
        ],
        out_specs=[pl.BlockSpec(piece, lambda i: (i, 0, 0, 0))] * 4,
        out_shape=[jax.ShapeDtypeStruct((2,) + piece[1:], BF)] * 4,
        scratch_shapes=[pltpu.VMEM((4,) + piece[1:], BF)],
        compiler_params=params(),
        name="query_value_proj",
    )(place, normed, weight)


def over_x(pieces):
    return [pieces[0], send(pieces[3], dx=3), send(pieces[2], dx=2), send(pieces[1], dx=1)]


def scores_kernel(place_ref, q0_ref, q1_ref, *refs):
    keys, out_ref = refs[:16], refs[16]

    def source(xh, xl):
        return (xh * 2 + xl + 4 - place_ref[X]) % 4

    def query_rows(xh):
        return jnp.concatenate(
            [q[source(xh, xl), rp] for q in (q0_ref, q1_ref) for xl in range(2) for rp in range(2)], axis=1
        )

    def key_rows(d, xh):
        return jnp.concatenate(
            [keys[k * 8 + d * 2 + rp][source(xh, xl)] for k in range(2) for xl in range(2) for rp in range(2)], axis=1
        )

    left = jnp.concatenate([query_rows(0), query_rows(1)], axis=0)
    for d in range(4):
        right = jnp.concatenate([key_rows(d, 0), key_rows(d, 1)], axis=0)
        out_ref[:, 0, :, d * 256 : (d + 1) * 256] = mm_t(left, right).reshape(4, 32, 256)


def partial_scores(place, q0, q1, k0, k1):
    q_spec = pl.BlockSpec((4, 2, 64, 128), lambda h: (0, 0, 0, h))
    k_spec = pl.BlockSpec((4, 128, 128), lambda h: (0, 0, h))
    return pl.pallas_call(
        scores_kernel,
        grid=(3,),
        in_specs=[SCALARS, q_spec, q_spec] + [k_spec] * 16,
        out_specs=pl.BlockSpec((4, 1, 32, 1024), lambda h: (0, h, 0, 0)),
        out_shape=jax.ShapeDtypeStruct((4, 3, 32, 1024), F32),
        compiler_params=params(),
        name="partial_scores",
    )(place, q0, q1, *k0, *k1)


def softmax_kernel(scale, parts_ref, out_ref):
    tied = (parts_ref[0] + parts_ref[1] + parts_ref[2] + parts_ref[3]) * scale
    expo = jnp.exp(tied - jnp.max(tied, axis=-1, keepdims=True))
    out_ref[...] = (expo / jnp.sum(expo, axis=-1, keepdims=True)).astype(BF)


def row_softmax(parts, scale):
    return pl.pallas_call(
        lambda *refs: softmax_kernel(scale, *refs),
        grid=(3,),
        in_specs=[pl.BlockSpec((4, 1, 32, 1024), lambda h: (0, h, 0, 0))],
        out_specs=pl.BlockSpec((1, 32, 1024), lambda h: (h, 0, 0)),
        out_shape=jax.ShapeDtypeStruct((3, 32, 1024), BF),
        compiler_params=params(),
        name="row_softmax",
    )(parts)


def mix_kernel(place_ref, w0_ref, w1_ref, w2_ref, w3_ref, v0_ref, v1_ref, out_ref, weights):
    for d, w in enumerate((w0_ref, w1_ref, w2_ref, w3_ref)):
        share = (place_ref[Y] + d) % 4
        weights[pl.ds(pl.multiple_of(share * 32, 32), 32), :] = w[0]
    for k, v in enumerate((v0_ref, v1_ref)):
        owner = (place_ref[CORE] + k) % 2
        for xl in range(2):
            right = []
            for dz in (0, 3, 1, 2):
                z = (place_ref[Z] + dz) % 4
                for xh in range(2):
                    x = (xh * 2 + xl + 4 - place_ref[X]) % 4
                    right.append(jnp.concatenate([v[z, x, 0], v[z, x, 1]], axis=1))
            mixed = mm(weights[...], jnp.concatenate(right, axis=0))
            pair = jnp.concatenate(
                [mixed[:, :128].reshape(16, 8, 128), mixed[:, 128:].reshape(16, 8, 128)], axis=1
            )
            out_ref[:, pl.ds(owner, 1), xl * 16 : (xl + 1) * 16, :] = pair.astype(BF)[:, None]


def row_mix(place, weights, v0, v1):
    w_spec = pl.BlockSpec((1, 32, 1024), lambda h: (h, 0, 0))
    v_spec = pl.BlockSpec((4, 4, 2, 128, 128), lambda h: (0, 0, 0, 0, h))
    return pl.pallas_call(
        mix_kernel,
        grid=(3,),
        in_specs=[SCALARS] + [w_spec] * 4 + [v_spec] * 2,
        out_specs=pl.BlockSpec((16, 2, 32, 128), lambda h: (0, 0, 0, h)),
        out_shape=jax.ShapeDtypeStruct((16, 2, 32, 384), BF),
        scratch_shapes=[pltpu.VMEM((128, 1024), BF)],
        compiler_params=params(),
        name="row_mix",
    )(place, *weights, v0, v1)


def column_kernel(
    mix_ref, x_ref, gain_col_ref, gain_ffn_ref, exit_row_hbm, attend_hbm, exit_col_hbm, expand_hbm, shrink_hbm,
    out_ref, exit_row, attend, exit_col, expand, shrink, qkv, stream, col_mix, sems,
):
    copies = [
        pltpu.make_async_copy(src, dst, sems.at[i])
        for i, (src, dst) in enumerate(
            [
                (exit_row_hbm, exit_row),
                (attend_hbm, attend),
                (exit_col_hbm, exit_col),
                (expand_hbm, expand),
                (shrink_hbm, shrink),
            ]
        )
    ]
    for copy in copies:
        copy.start()

    low = lax.broadcasted_iota(jnp.int32, (64, 128), 1) < E
    halves = ([], [])
    for y in range(4):
        tiles = ([], [])
        for t in range(6):
            (g0, h0), (g1, h1) = divmod(2 * t, 3), divmod(2 * t + 1, 3)
            a = mix_ref[g0 * 4 + y, :, h0 * 128 : (h0 + 1) * 128].astype(F32)
            b = mix_ref[g1 * 4 + y, :, h1 * 128 : (h1 + 1) * 128].astype(F32)
            tiles[0].append(jnp.where(low, a, pltpu.roll(b, E, 1)).astype(BF))
            tiles[1].append(jnp.where(low, pltpu.roll(a, E, 1), b).astype(BF))
        for k in range(2):
            halves[k].append(jnp.concatenate(tiles[k], axis=1))
    copies[0].wait()
    exits = [mm(jnp.concatenate(halves[k], axis=0), exit_row[...]).reshape(32, 1, 8, 768) for k in range(2)]
    exits = jnp.concatenate(exits, axis=1).reshape(512, 768)
    x = jnp.concatenate([x_ref[(xl * 4 + y) * 2 + c] for y in range(4) for c in range(2) for xl in range(2)], axis=0)
    stream[...] = x.astype(F32) + exits

    place = lax.broadcasted_iota(jnp.int32, (512, 512), 0)
    token = lax.broadcasted_iota(jnp.int32, (512, 512), 1)
    by_column = ((place % 64) * 8 + place // 64 == token).astype(F32).astype(BF)
    by_token = ((token % 64) * 8 + token // 64 == place).astype(F32).astype(BF)
    normed = mm(by_column, normalize(stream[...], gain_col_ref[...][None, :])).astype(BF)
    copies[1].wait()
    qkv[...] = mm(normed, attend[...]).astype(BF)
    group = lax.broadcasted_iota(jnp.int32, (256, 256), 0) // E == lax.broadcasted_iota(jnp.int32, (256, 256), 1) // E
    group = group.astype(F32).astype(BF)
    segment = lax.broadcasted_iota(jnp.int32, (64, 128), 1) < E
    for c in range(8):
        for g in range(3):
            rows, lanes = slice(c * 64, (c + 1) * 64), g * 256
            q = qkv[rows, lanes : lanes + 256]
            k = qkv[rows, 768 + lanes : 768 + lanes + 256]
            v = qkv[rows, 1536 + lanes : 1536 + lanes + 256]
            k = jnp.concatenate([k] * 4, axis=0) * group
            v = jnp.concatenate([v] * 4, axis=0) * group
            scores = mm_t(q, k) * (E ** -0.5)
            weights = []
            for half in range(2):
                s = scores[:, half * 128 : (half + 1) * 128]
                top0 = jnp.max(jnp.where(segment, s, -jnp.inf), axis=-1, keepdims=True)
                top1 = jnp.max(jnp.where(segment, -jnp.inf, s), axis=-1, keepdims=True)
                expo = jnp.exp(s - jnp.where(segment, top0, top1))
                sum0 = jnp.sum(jnp.where(segment, expo, 0.0), axis=-1, keepdims=True)
                sum1 = jnp.sum(jnp.where(segment, 0.0, expo), axis=-1, keepdims=True)
                weights.append((expo / jnp.where(segment, sum0, sum1)).astype(BF))
            col_mix[rows, lanes : lanes + 256] = mm(jnp.concatenate(weights, axis=1), v).astype(BF)
    mixed = mm(by_token, col_mix[...]).astype(BF)
    copies[2].wait()
    stream[...] += mm(mixed, exit_col[...])

    normed = normalize(stream[...], gain_ffn_ref[...][None, :])
    copies[3].wait()
    copies[4].wait()
    for f in range(6):
        cols = slice(f * 512, (f + 1) * 512)
        pre = mm(normed, expand[:, cols])
        hidden = (0.5 * pre * (1.0 + lax.erf(pre * math.sqrt(0.5)))).astype(BF)
        stream[...] += mm(hidden, shrink[cols, :])
    done = stream[...].astype(BF)
    for i, (y, c, xl) in enumerate((y, c, xl) for y in range(4) for c in range(2) for xl in range(2)):
        out_ref[(xl * 4 + y) * 2 + c] = done[i * 32 : (i + 1) * 32, :]


def column_part(mix, x, gain_col, gain_ffn, exit_row, attend, exit_col, expand, shrink):
    whole = pl.BlockSpec(memory_space=pltpu.VMEM)
    hbm = pl.BlockSpec(memory_space=pl.ANY)
    return pl.pallas_call(
        column_kernel,
        in_specs=[whole] * 4 + [hbm] * 5,
        out_specs=whole,
        out_shape=jax.ShapeDtypeStruct((16, 32, 768), BF),
        scratch_shapes=[pltpu.VMEM(w.shape, BF) for w in (exit_row, attend, exit_col, expand, shrink)]
        + [
            pltpu.VMEM((512, 2304), BF),
            pltpu.VMEM((512, 768), F32),
            pltpu.VMEM((512, 768), BF),
            pltpu.SemaphoreType.DMA((5,)),
        ],
        compiler_params=params(),
        name="column_part",
    )(mix, x, gain_col, gain_ffn, exit_row, attend, exit_col, expand, shrink)


def local(
    embeddings,
    gain_row,
    attend_row,
    exit_row,
    gain_col,
    attend_col,
    exit_col,
    gain_ffn,
    expand,
    shrink,
):
    seq, col = lax.axis_index("seq"), lax.axis_index("col")
    core, y, z = seq % 2, seq // 2 % 4, col // 2
    place = jnp.stack([core, col % 2 * 2 + seq // 8, y, z]).astype(jnp.int32)
    scale = E ** (-0.5) / math.sqrt(embeddings.shape[0] * lax.axis_size("seq"))

    normed, *keys = key_proj(place, embeddings.reshape(512, 768), gain_row, attend_row)
    keys = over_x(keys)
    queries_values = query_value_proj(place, normed, attend_row)
    x = embeddings.reshape(4, 2, 8, 8, 768).transpose(2, 1, 0, 3, 4).reshape(16, 32, 768)
    even, odd = (jnp.stack([k[rp] for k in keys]) for rp in range(2))
    even, odd, x, queries_values = lax.optimization_barrier((even, odd, x, queries_values))

    even_below, odd_above = send(even, dz=1), send(odd, dz=3)
    odd_below, even_above = send(odd, dz=1), send(even, dz=3)
    queries_values = over_x(queries_values)
    x = lax.all_to_all(x, "seq", split_axis=0, concat_axis=0, tiled=True)
    even_below, odd_above, x = lax.optimization_barrier((even_below, odd_above, x))
    even_far, odd_far = send(even_below, dz=1), send(odd_above, dz=3)
    keys0 = [even, odd, even_below, odd_below, even_above, odd_above, even_far, odd_far]
    keys1 = [to_other_core(k) for k in keys0]

    queries = jnp.stack([qv[0] for qv in queries_values])
    values = jnp.stack([qv[1] for qv in queries_values])
    queries0 = lax.dynamic_slice_in_dim(queries, core * 64, 64, axis=2)
    queries1 = to_other_core(lax.dynamic_slice_in_dim(queries, (1 - core) * 64, 64, axis=2))
    values, keys0[6], keys0[7] = lax.optimization_barrier((values, keys0[6], keys0[7]))
    values0 = gather(values, Z_RINGS)

    scores = partial_scores(place, queries0, queries1, keys0, keys1)
    weights = row_softmax(swap(scores, Y_RINGS), scale)
    weights, values0 = lax.optimization_barrier((weights, values0))
    weights = [weights] + [send(weights, dy=dy) for dy in (3, 2, 1)]
    mix = row_mix(place, weights, values0, to_other_core(values0))
    mix = swap(mix, PLANES).reshape(16, 64, 384)

    out = column_part(mix, x, gain_col, gain_ffn, exit_row, attend_col, exit_col, expand, shrink)
    out = lax.all_to_all(out, "seq", split_axis=0, concat_axis=0, tiled=True)
    return out.reshape(8, 2, 4, 8, 768).transpose(2, 1, 0, 3, 4).reshape(4, 128, 768)


def solution(mesh):
    in_specs = (P("seq", "col", None), P(), P(), P(), P(), P(), P(), P(), P(), P())
    out_specs = P("seq", "col", None)
    return jax.shard_map(local, mesh=mesh, in_specs=in_specs, out_specs=out_specs, check_vma=False)
```

```python
import math

import jax
import jax.numpy as jnp
from jax import lax
from jax.experimental import pallas as pl
from jax.experimental.pallas import tpu as pltpu
from jax.sharding import PartitionSpec as P

AXES = ("seq", "col")
HEADS = 12
E = 64
BF = jnp.bfloat16
F32 = jnp.float32
VMEM_LIMIT = 56 * 1024 * 1024


def device(xl, y, c, z, xh):
    return ((xl * 4 + y) * 2 + c) * 8 + z * 2 + xh


R2, R4 = range(2), range(4)
Y_RINGS = [[device(xl, y, c, z, xh) for y in R4] for xl in R2 for c in R2 for z in R4 for xh in R2]
Z_RINGS = [[device(xl, y, c, z, xh) for z in R4] for xl in R2 for y in R4 for c in R2 for xh in R2]
X_RINGS = [[device(xl, y, c, z, xh) for xh in R2 for xl in R2] for y in R4 for c in R2 for z in R4]
PLANES = [[device(xl, y, c, z, xh) for xh in R2 for xl in R2 for y in R4] for c in R2 for z in R4]


def shifts(dx=0, dy=0, dz=0, dc=0):
    pairs = []
    for x in R4:
        for y in R4:
            for c in R2:
                for z in R4:
                    to = ((x + dx) % 4, (y + dy) % 4, (c + dc) % 2, (z + dz) % 4)
                    pairs.append((device(x % 2, y, c, z, x // 2), device(to[0] % 2, *to[1:], to[0] // 2)))
    return pairs


def params():
    return pltpu.CompilerParams(vmem_limit_bytes=VMEM_LIMIT)


def swap(array, groups):
    return lax.all_to_all(array, AXES, split_axis=0, concat_axis=0, tiled=True, axis_index_groups=groups)


def gather(array, groups):
    return lax.all_gather(array, AXES, axis=0, tiled=False, axis_index_groups=groups)


def send(array, **by):
    return lax.ppermute(array, AXES, shifts(**by))


def to_other_core(array):
    return send(array, dc=1)


def mm(a, b):
    return jnp.dot(a, b, preferred_element_type=F32)


def mm_t(a, b):
    return lax.dot_general(a, b, (((1,), (1,)), ((), ())), preferred_element_type=F32)


def normalize(stream, gain):
    mean = jnp.mean(stream, axis=-1, keepdims=True)
    centred = stream - mean
    var = jnp.mean(centred * centred, axis=-1, keepdims=True)
    return (centred * lax.rsqrt(var + 1e-05) * gain).astype(BF)


CORE, X, Y, Z = range(4)
SCALARS = pl.BlockSpec(memory_space=pltpu.SMEM)


def write_pairs(normed, weight, out):
    low = lax.broadcasted_iota(jnp.int32, (128, 128), 1) < E
    for rp in range(2):
        first = mm(normed[2 * rp * 128 : (2 * rp + 1) * 128, :], weight)
        second = mm(normed[(2 * rp + 1) * 128 : (2 * rp + 2) * 128, :], weight)
        for t in range(6):
            a, b = first[:, t * 128 : (t + 1) * 128], second[:, t * 128 : (t + 1) * 128]
            pair = (
                jnp.where(low, a, pltpu.roll(b, E, 1)),
                jnp.where(low, pltpu.roll(a, E, 1), b),
            )
            for k in range(2):
                g, h = (2 * t + k) // 3, (2 * t + k) % 3
                out[g, rp, :, h * 128 : (h + 1) * 128] = pair[k].astype(BF)


def key_kernel(place_ref, x_ref, gain_ref, w_ref, normed_ref, *refs):
    normed_ref[...] = normalize(x_ref[...].astype(F32), gain_ref[...][None, :])
    outs, pieces = refs[:4], refs[4]
    write_pairs(normed_ref[...], w_ref[...], pieces)
    for s, out in enumerate(outs):
        out[...] = pieces[(place_ref[X] + s) % 4]


def key_proj(place, x, gain, weight):
    piece = (2, 128, 384)
    return pl.pallas_call(
        key_kernel,
        grid=(1,),
        in_specs=[
            SCALARS,
            pl.BlockSpec((512, 768), lambda i: (0, 0)),
            pl.BlockSpec((768,), lambda i: (0,)),
            pl.BlockSpec((768, 768), lambda i: (0, 1)),
        ],
        out_specs=[pl.BlockSpec((512, 768), lambda i: (0, 0))] + [pl.BlockSpec(piece, lambda i: (0, 0, 0))] * 4,
        out_shape=[jax.ShapeDtypeStruct((512, 768), BF)] + [jax.ShapeDtypeStruct(piece, BF)] * 4,
        scratch_shapes=[pltpu.VMEM((4,) + piece, BF)],
        compiler_params=params(),
        name="key_proj",
    )(place, x, gain, weight)


def query_value_kernel(normed_ref, w_ref, out_ref):
    write_pairs(normed_ref[...], w_ref[...], out_ref.at[:, 0])


def query_value_proj(normed, weight):
    return pl.pallas_call(
        query_value_kernel,
        grid=(2,),
        in_specs=[
            pl.BlockSpec((512, 768), lambda i: (0, 0)),
            pl.BlockSpec((768, 768), lambda i: (0, 2 * i)),
        ],
        out_specs=pl.BlockSpec((4, 1, 2, 128, 384), lambda i: (0, i, 0, 0, 0)),
        out_shape=jax.ShapeDtypeStruct((4, 2, 2, 128, 384), BF),
        compiler_params=params(),
        name="query_value_proj",
    )(normed, weight)


def over_x(pieces):
    return [pieces[0], send(pieces[3], dx=3), send(pieces[2], dx=2), send(pieces[1], dx=1)]


def scores_kernel(place_ref, q0_ref, q1_ref, *refs):
    keys, out_ref = (refs[:4], refs[4:8]), refs[8]

    def query_rows(xh):
        return jnp.concatenate(
            [q[xh * 2 + xl, rp] for q in (q0_ref, q1_ref) for xl in range(2) for rp in range(2)], axis=1
        )

    def key_rows(d, xh):
        sources = [(xh * 2 + xl + 4 - place_ref[X]) % 4 for xl in range(2)]
        return jnp.concatenate([keys[k][d][x, rp] for k in range(2) for x in sources for rp in range(2)], axis=1)

    left = jnp.concatenate([query_rows(0), query_rows(1)], axis=0)
    for d in range(4):
        right = jnp.concatenate([key_rows(d, 0), key_rows(d, 1)], axis=0)
        out_ref[:, 0, :, d * 256 : (d + 1) * 256] = mm_t(left, right).reshape(4, 32, 256)


def partial_scores(place, q0, q1, k0, k1):
    q_spec = pl.BlockSpec((4, 2, 64, 128), lambda h: (0, 0, 0, h))
    k_spec = pl.BlockSpec((4, 2, 128, 128), lambda h: (0, 0, 0, h))
    return pl.pallas_call(
        scores_kernel,
        grid=(3,),
        in_specs=[SCALARS, q_spec, q_spec] + [k_spec] * 8,
        out_specs=pl.BlockSpec((4, 1, 32, 1024), lambda h: (0, h, 0, 0)),
        out_shape=jax.ShapeDtypeStruct((4, 3, 32, 1024), F32),
        compiler_params=params(),
        name="partial_scores",
    )(place, q0, q1, *k0, *k1)


def softmax_kernel(scale, parts_ref, out_ref):
    tied = (parts_ref[0] + parts_ref[1] + parts_ref[2] + parts_ref[3]) * scale
    expo = jnp.exp(tied - jnp.max(tied, axis=-1, keepdims=True))
    out_ref[...] = (expo / jnp.sum(expo, axis=-1, keepdims=True)).astype(BF)


def row_softmax(parts, scale):
    return pl.pallas_call(
        lambda *refs: softmax_kernel(scale, *refs),
        grid=(3,),
        in_specs=[pl.BlockSpec((4, 1, 32, 1024), lambda h: (0, h, 0, 0))],
        out_specs=pl.BlockSpec((1, 32, 1024), lambda h: (h, 0, 0)),
        out_shape=jax.ShapeDtypeStruct((3, 32, 1024), BF),
        compiler_params=params(),
        name="row_softmax",
    )(parts)


def mix_kernel(place_ref, w0_ref, w1_ref, w2_ref, w3_ref, v0_ref, v1_ref, out_ref, weights):
    for d, w in enumerate((w0_ref, w1_ref, w2_ref, w3_ref)):
        share = (place_ref[Y] + d) % 4
        weights[pl.ds(pl.multiple_of(share * 32, 32), 32), :] = w[0]
    for k, v in enumerate((v0_ref, v1_ref)):
        owner = (place_ref[CORE] + k) % 2
        for xl in range(2):
            right = []
            for dz in (0, 3, 1, 2):
                z = (place_ref[Z] + dz) % 4
                for x in (xl, 2 + xl):
                    right.append(jnp.concatenate([v[z, x, 0], v[z, x, 1]], axis=1))
            mixed = mm(weights[...], jnp.concatenate(right, axis=0))
            pair = jnp.concatenate(
                [mixed[:, :128].reshape(16, 8, 128), mixed[:, 128:].reshape(16, 8, 128)], axis=1
            )
            out_ref[:, pl.ds(owner, 1), xl * 16 : (xl + 1) * 16, :] = pair.astype(BF)[:, None]


def row_mix(place, weights, v0, v1):
    w_spec = pl.BlockSpec((1, 32, 1024), lambda h: (h, 0, 0))
    v_spec = pl.BlockSpec((4, 4, 2, 128, 128), lambda h: (0, 0, 0, 0, h))
    return pl.pallas_call(
        mix_kernel,
        grid=(3,),
        in_specs=[SCALARS] + [w_spec] * 4 + [v_spec] * 2,
        out_specs=pl.BlockSpec((16, 2, 32, 128), lambda h: (0, 0, 0, h)),
        out_shape=jax.ShapeDtypeStruct((16, 2, 32, 384), BF),
        scratch_shapes=[pltpu.VMEM((128, 1024), BF)],
        compiler_params=params(),
        name="row_mix",
    )(place, *weights, v0, v1)


def column_kernel(
    mix_ref, x_ref, gain_col_ref, gain_ffn_ref, exit_row_hbm, attend_hbm, exit_col_hbm, expand_hbm, shrink_hbm,
    out_ref, exit_row, attend, exit_col, expand, shrink, qkv, stream, col_mix, sems,
):
    copies = [
        pltpu.make_async_copy(src, dst, sems.at[i])
        for i, (src, dst) in enumerate(
            [
                (exit_row_hbm, exit_row),
                (attend_hbm, attend),
                (exit_col_hbm, exit_col),
                (expand_hbm, expand),
                (shrink_hbm, shrink),
            ]
        )
    ]
    for copy in copies:
        copy.start()

    low = lax.broadcasted_iota(jnp.int32, (64, 128), 1) < E
    halves = ([], [])
    for y in range(4):
        tiles = ([], [])
        for t in range(6):
            (g0, h0), (g1, h1) = divmod(2 * t, 3), divmod(2 * t + 1, 3)
            a = mix_ref[g0 * 4 + y, :, h0 * 128 : (h0 + 1) * 128].astype(F32)
            b = mix_ref[g1 * 4 + y, :, h1 * 128 : (h1 + 1) * 128].astype(F32)
            tiles[0].append(jnp.where(low, a, pltpu.roll(b, E, 1)).astype(BF))
            tiles[1].append(jnp.where(low, pltpu.roll(a, E, 1), b).astype(BF))
        for k in range(2):
            halves[k].append(jnp.concatenate(tiles[k], axis=1))
    copies[0].wait()
    exits = [mm(jnp.concatenate(halves[k], axis=0), exit_row[...]).reshape(32, 1, 8, 768) for k in range(2)]
    exits = jnp.concatenate(exits, axis=1).reshape(512, 768)
    x = jnp.concatenate([x_ref[(xl * 4 + y) * 2 + c] for y in range(4) for c in range(2) for xl in range(2)], axis=0)
    stream[...] = x.astype(F32) + exits

    place = lax.broadcasted_iota(jnp.int32, (512, 512), 0)
    token = lax.broadcasted_iota(jnp.int32, (512, 512), 1)
    by_column = ((place % 64) * 8 + place // 64 == token).astype(F32).astype(BF)
    by_token = ((token % 64) * 8 + token // 64 == place).astype(F32).astype(BF)
    normed = mm(by_column, normalize(stream[...], gain_col_ref[...][None, :])).astype(BF)
    copies[1].wait()
    qkv[...] = mm(normed, attend[...]).astype(BF)
    group = lax.broadcasted_iota(jnp.int32, (256, 256), 0) // E == lax.broadcasted_iota(jnp.int32, (256, 256), 1) // E
    group = group.astype(F32).astype(BF)
    segment = lax.broadcasted_iota(jnp.int32, (64, 128), 1) < E
    for c in range(8):
        for g in range(3):
            rows, lanes = slice(c * 64, (c + 1) * 64), g * 256
            q = qkv[rows, lanes : lanes + 256]
            k = qkv[rows, 768 + lanes : 768 + lanes + 256]
            v = qkv[rows, 1536 + lanes : 1536 + lanes + 256]
            k = jnp.concatenate([k] * 4, axis=0) * group
            v = jnp.concatenate([v] * 4, axis=0) * group
            scores = mm_t(q, k) * (E ** -0.5)
            weights = []
            for half in range(2):
                s = scores[:, half * 128 : (half + 1) * 128]
                top0 = jnp.max(jnp.where(segment, s, -jnp.inf), axis=-1, keepdims=True)
                top1 = jnp.max(jnp.where(segment, -jnp.inf, s), axis=-1, keepdims=True)
                expo = jnp.exp(s - jnp.where(segment, top0, top1))
                sum0 = jnp.sum(jnp.where(segment, expo, 0.0), axis=-1, keepdims=True)
                sum1 = jnp.sum(jnp.where(segment, 0.0, expo), axis=-1, keepdims=True)
                weights.append((expo / jnp.where(segment, sum0, sum1)).astype(BF))
            col_mix[rows, lanes : lanes + 256] = mm(jnp.concatenate(weights, axis=1), v).astype(BF)
    mixed = mm(by_token, col_mix[...]).astype(BF)
    copies[2].wait()
    stream[...] += mm(mixed, exit_col[...])

    normed = normalize(stream[...], gain_ffn_ref[...][None, :])
    copies[3].wait()
    copies[4].wait()
    for f in range(6):
        cols = slice(f * 512, (f + 1) * 512)
        pre = mm(normed, expand[:, cols])
        hidden = (0.5 * pre * (1.0 + lax.erf(pre * math.sqrt(0.5)))).astype(BF)
        stream[...] += mm(hidden, shrink[cols, :])
    done = stream[...].astype(BF)
    for i, (y, c, xl) in enumerate((y, c, xl) for y in range(4) for c in range(2) for xl in range(2)):
        out_ref[(xl * 4 + y) * 2 + c] = done[i * 32 : (i + 1) * 32, :]


def column_part(mix, x, gain_col, gain_ffn, exit_row, attend, exit_col, expand, shrink):
    whole = pl.BlockSpec(memory_space=pltpu.VMEM)
    hbm = pl.BlockSpec(memory_space=pl.ANY)
    return pl.pallas_call(
        column_kernel,
        in_specs=[whole] * 4 + [hbm] * 5,
        out_specs=whole,
        out_shape=jax.ShapeDtypeStruct((16, 32, 768), BF),
        scratch_shapes=[pltpu.VMEM(w.shape, BF) for w in (exit_row, attend, exit_col, expand, shrink)]
        + [
            pltpu.VMEM((512, 2304), BF),
            pltpu.VMEM((512, 768), F32),
            pltpu.VMEM((512, 768), BF),
            pltpu.SemaphoreType.DMA((5,)),
        ],
        compiler_params=params(),
        name="column_part",
    )(mix, x, gain_col, gain_ffn, exit_row, attend, exit_col, expand, shrink)


def local(
    embeddings,
    gain_row,
    attend_row,
    exit_row,
    gain_col,
    attend_col,
    exit_col,
    gain_ffn,
    expand,
    shrink,
):
    seq, col = lax.axis_index("seq"), lax.axis_index("col")
    core, y, z = seq % 2, seq // 2 % 4, col // 2
    place = jnp.stack([core, col % 2 * 2 + seq // 8, y, z]).astype(jnp.int32)
    scale = E ** (-0.5) / math.sqrt(embeddings.shape[0] * lax.axis_size("seq"))

    normed, *keys = key_proj(place, embeddings.reshape(512, 768), gain_row, attend_row)
    keys = over_x(keys)
    queries_values = query_value_proj(normed, attend_row)
    x = embeddings.reshape(4, 2, 8, 8, 768).transpose(2, 1, 0, 3, 4).reshape(16, 32, 768)
    keys, queries_values = lax.optimization_barrier((jnp.stack(keys), queries_values))

    keys0 = [keys] + [send(keys, dz=dz) for dz in (1, 3, 2)]
    keys1 = [to_other_core(k) for k in keys0]
    queries_values, x = lax.optimization_barrier((swap(queries_values, X_RINGS), x))
    x = lax.all_to_all(x, "seq", split_axis=0, concat_axis=0, tiled=True)
    queries, values = queries_values[:, 0], queries_values[:, 1]
    queries0 = lax.dynamic_slice_in_dim(queries, core * 64, 64, axis=2)
    queries1 = to_other_core(lax.dynamic_slice_in_dim(queries, (1 - core) * 64, 64, axis=2))
    values = lax.optimization_barrier((values, queries1, x, *keys0))[0]
    values0 = gather(values, Z_RINGS)

    scores = partial_scores(place, queries0, queries1, keys0, keys1)
    weights = row_softmax(swap(scores, Y_RINGS), scale)
    weights, values0 = lax.optimization_barrier((weights, values0))
    weights = [weights] + [send(weights, dy=dy) for dy in (3, 2, 1)]
    mix = row_mix(place, weights, values0, to_other_core(values0))
    mix = swap(mix, PLANES).reshape(16, 64, 384)

    out = column_part(mix, x, gain_col, gain_ffn, exit_row, attend_col, exit_col, expand, shrink)
    out = lax.all_to_all(out, "seq", split_axis=0, concat_axis=0, tiled=True)
    return out.reshape(8, 2, 4, 8, 768).transpose(2, 1, 0, 3, 4).reshape(4, 128, 768)


def solution(mesh):
    in_specs = (P("seq", "col", None), P(), P(), P(), P(), P(), P(), P(), P(), P())
    out_specs = P("seq", "col", None)
    return jax.shard_map(local, mesh=mesh, in_specs=in_specs, out_specs=out_specs, check_vma=False)
```

```python
import math

import jax
import jax.numpy as jnp
from jax import lax
from jax.experimental import pallas as pl
from jax.experimental.pallas import tpu as pltpu
from jax.sharding import PartitionSpec as P

AXES = ("seq", "col")
HEADS = 12
E = 64
BF = jnp.bfloat16
F32 = jnp.float32


def device(xl, y, c, z, xh):
    return ((xl * 4 + y) * 2 + c) * 8 + z * 2 + xh


R2, R4 = range(2), range(4)
Y_RINGS = [[device(xl, y, c, z, xh) for y in R4] for xl in R2 for c in R2 for z in R4 for xh in R2]
Z_RINGS = [[device(xl, y, c, z, xh) for z in R4] for xl in R2 for y in R4 for c in R2 for xh in R2]
X_RINGS = [[device(xl, y, c, z, xh) for xh in R2 for xl in R2] for y in R4 for c in R2 for z in R4]
PLANES = [[device(xl, y, c, z, xh) for xh in R2 for xl in R2 for y in R4] for c in R2 for z in R4]


def shifts(dx=0, dy=0, dz=0, dc=0):
    pairs = []
    for x in R4:
        for y in R4:
            for c in R2:
                for z in R4:
                    to = ((x + dx) % 4, (y + dy) % 4, (c + dc) % 2, (z + dz) % 4)
                    pairs.append((device(x % 2, y, c, z, x // 2), device(to[0] % 2, *to[1:], to[0] // 2)))
    return pairs


def params(mib):
    return pltpu.CompilerParams(vmem_limit_bytes=mib * 1024 * 1024)


def swap(array, groups):
    return lax.all_to_all(array, AXES, split_axis=0, concat_axis=0, tiled=True, axis_index_groups=groups)


def gather(array, groups):
    return lax.all_gather(array, AXES, axis=0, tiled=False, axis_index_groups=groups)


def send(array, **by):
    return lax.ppermute(array, AXES, shifts(**by))


def to_other_core(array):
    return send(array, dc=1)


def mm(a, b):
    return jnp.dot(a, b, preferred_element_type=F32)


def mm_t(a, b):
    return lax.dot_general(a, b, (((1,), (1,)), ((), ())), preferred_element_type=F32)


def centre(stream):
    mean = jnp.mean(stream, axis=-1, keepdims=True)
    centred = stream - mean
    var = jnp.mean(centred * centred, axis=-1, keepdims=True)
    return centred * lax.rsqrt(var + 1e-05)


def normalize(stream, gain):
    return (centre(stream) * gain).astype(BF)


CORE, X, Y, Z = range(4)
SCALARS = pl.BlockSpec(memory_space=pltpu.SMEM)


def write_pairs(normed, weight, out):
    low = lax.broadcasted_iota(jnp.int32, (128, 128), 1) < E
    for rp in range(2):
        first = mm(normed[2 * rp * 128 : (2 * rp + 1) * 128, :], weight)
        second = mm(normed[(2 * rp + 1) * 128 : (2 * rp + 2) * 128, :], weight)
        for t in range(6):
            a, b = first[:, t * 128 : (t + 1) * 128], second[:, t * 128 : (t + 1) * 128]
            pair = (
                jnp.where(low, a, pltpu.roll(b, E, 1)),
                jnp.where(low, pltpu.roll(a, E, 1), b),
            )
            for k in range(2):
                g, h = (2 * t + k) // 3, (2 * t + k) % 3
                out[g, h, rp] = pair[k].astype(BF)


def key_kernel(place_ref, x_ref, gain_ref, w_ref, normed_ref, *refs):
    normed_ref[...] = normalize(x_ref[...].astype(F32), gain_ref[...][None, :])
    outs, pieces = refs[:4], refs[4]
    write_pairs(normed_ref[...], w_ref[...], pieces)
    for s, out in enumerate(outs):
        out[...] = pieces[(place_ref[X] + s) % 4]


def key_proj(place, x, gain, weight):
    piece = (3, 2, 128, 128)
    return pl.pallas_call(
        key_kernel,
        grid=(1,),
        in_specs=[
            SCALARS,
            pl.BlockSpec((512, 768), lambda i: (0, 0)),
            pl.BlockSpec((768,), lambda i: (0,)),
            pl.BlockSpec((768, 768), lambda i: (0, 1)),
        ],
        out_specs=[pl.BlockSpec((512, 768), lambda i: (0, 0))] + [pl.BlockSpec(piece, lambda i: (0, 0, 0, 0))] * 4,
        out_shape=[jax.ShapeDtypeStruct((512, 768), BF)] + [jax.ShapeDtypeStruct(piece, BF)] * 4,
        scratch_shapes=[pltpu.VMEM((4,) + piece, BF)],
        compiler_params=params(56),
        name="key_proj",
    )(place, x, gain, weight)


def query_value_kernel(normed_ref, w_ref, out_ref):
    write_pairs(normed_ref[...], w_ref[...], out_ref.at[:, 0])


def query_value_proj(normed, weight):
    return pl.pallas_call(
        query_value_kernel,
        grid=(2,),
        in_specs=[
            pl.BlockSpec((512, 768), lambda i: (0, 0)),
            pl.BlockSpec((768, 768), lambda i: (0, 2 * i)),
        ],
        out_specs=pl.BlockSpec((4, 1, 3, 2, 128, 128), lambda i: (0, i, 0, 0, 0, 0)),
        out_shape=jax.ShapeDtypeStruct((4, 2, 3, 2, 128, 128), BF),
        compiler_params=params(16),
        name="query_value_proj",
    )(normed, weight)


def over_x(pieces):
    return [pieces[0], send(pieces[3], dx=3), send(pieces[2], dx=2), send(pieces[1], dx=1)]


def scores_kernel(place_ref, q0_ref, q1_ref, *refs):
    blocks, out_ref = refs[:8], refs[8]
    for h in range(3):
        left = [
            jnp.concatenate(
                [
                    q[xh * 2 + xl, h, rp]
                    for q in (q0_ref, q1_ref)
                    for xl in range(2)
                    for rp in range(2)
                ],
                axis=1,
            )
            for xh in range(2)
        ]
        left = jnp.concatenate(left, axis=0)
        for d in range(4):
            right = [
                jnp.concatenate(
                    [
                        k[(xh * 2 + xl + 4 - place_ref[X]) % 4, h, rp]
                        for k in blocks[2 * d : 2 * d + 2]
                        for xl in range(2)
                        for rp in range(2)
                    ],
                    axis=1,
                )
                for xh in range(2)
            ]
            scores = mm_t(left, jnp.concatenate(right, axis=0))
            out_ref[:, h, :, d * 256 : (d + 1) * 256] = scores.reshape(4, 32, 256)


def partial_scores(place, q0, q1, k0, k1):
    vmem = pl.BlockSpec(memory_space=pltpu.VMEM)
    return pl.pallas_call(
        scores_kernel,
        in_specs=[SCALARS] + [vmem] * 10,
        out_specs=vmem,
        out_shape=jax.ShapeDtypeStruct((4, 3, 32, 1024), F32),
        compiler_params=params(14),
        name="partial_scores",
    )(place, q0, q1, *[k for pair in zip(k0, k1) for k in pair])


def softmax_kernel(scale, parts_ref, out_ref):
    tied = (parts_ref[0] + parts_ref[1] + parts_ref[2] + parts_ref[3]) * scale
    expo = jnp.exp(tied - jnp.max(tied, axis=-1, keepdims=True))
    out_ref[...] = (expo / jnp.sum(expo, axis=-1, keepdims=True)).astype(BF)


def row_softmax(parts, scale):
    return pl.pallas_call(
        lambda *refs: softmax_kernel(scale, *refs),
        in_specs=[pl.BlockSpec(memory_space=pltpu.VMEM)],
        out_specs=pl.BlockSpec(memory_space=pltpu.VMEM),
        out_shape=jax.ShapeDtypeStruct((3, 32, 1024), BF),
        compiler_params=params(8),
        name="row_softmax",
    )(parts)


def mix_kernel(place_ref, w0_ref, w1_ref, w2_ref, w3_ref, v0_ref, v1_ref, out_ref, weights, values, sem):
    copy = pltpu.make_async_copy(v0_ref, values, sem)
    copy.start()
    for d, w in enumerate((w0_ref, w1_ref, w2_ref, w3_ref)):
        share = (place_ref[Y] + d) % 4
        weights[:, pl.ds(pl.multiple_of(share * 32, 32), 32), :] = w[...]
    for k, v in ((1, v1_ref), (0, values)):
        if k == 0:
            copy.wait()
        owner = (place_ref[CORE] + k) % 2
        for xl in range(2):
            for h in range(3):
                right = [
                    jnp.concatenate([v[(place_ref[Z] + dz) % 4, xh * 2 + xl, h, rp] for rp in range(2)], axis=1)
                    for dz in (0, 3, 1, 2)
                    for xh in range(2)
                ]
                mixed = mm(weights[h], jnp.concatenate(right, axis=0))
                pair = jnp.concatenate(
                    [mixed[:, :128].reshape(16, 8, 128), mixed[:, 128:].reshape(16, 8, 128)], axis=1
                )
                out_ref[:, h, pl.ds(owner, 1), xl * 16 : (xl + 1) * 16, :] = pair.astype(BF)[:, None]


def row_mix(place, weights, v0, v1):
    vmem = pl.BlockSpec(memory_space=pltpu.VMEM)
    return pl.pallas_call(
        mix_kernel,
        in_specs=[SCALARS] + [vmem] * 4 + [pl.BlockSpec(memory_space=pltpu.HBM), vmem],
        out_specs=vmem,
        out_shape=jax.ShapeDtypeStruct((16, 3, 2, 32, 128), BF),
        scratch_shapes=[pltpu.VMEM((3, 128, 1024), BF), pltpu.VMEM(v0.shape, BF), pltpu.SemaphoreType.DMA],
        compiler_params=params(18),
        name="row_mix",
    )(place, *weights, v0, v1)


def column_kernel(
    mix_ref, x_ref, gain_col_ref, gain_ffn_ref, exit_row, attend, exit_col, expand_hbm, shrink_hbm,
    out_ref, qkv, stream, scratch, expand, shrink, sems,
):
    copies = [
        pltpu.make_async_copy(expand_hbm, expand, sems.at[0]),
        pltpu.make_async_copy(shrink_hbm, shrink, sems.at[1]),
    ]
    for copy in copies:
        copy.start()
    low = lax.broadcasted_iota(jnp.int32, (64, 128), 1) < E
    halves = ([], [])
    for y in range(4):
        tiles = ([], [])
        for t in range(6):
            (g0, h0), (g1, h1) = divmod(2 * t, 3), divmod(2 * t + 1, 3)
            a = mix_ref[g0 * 4 + y, h0].astype(F32)
            b = mix_ref[g1 * 4 + y, h1].astype(F32)
            tiles[0].append(jnp.where(low, a, pltpu.roll(b, E, 1)).astype(BF))
            tiles[1].append(jnp.where(low, pltpu.roll(a, E, 1), b).astype(BF))
        for k in range(2):
            halves[k].append(jnp.concatenate(tiles[k], axis=1))
    exits = [mm(jnp.concatenate(halves[k], axis=0), exit_row[...]).reshape(32, 1, 8, 768) for k in range(2)]
    exits = jnp.concatenate(exits, axis=1).reshape(512, 768)
    x = jnp.concatenate([x_ref[(xl * 4 + y) * 2 + c] for y in range(4) for c in range(2) for xl in range(2)], axis=0)
    stream[...] = x.astype(F32) + exits

    normed = centre(stream[...]) * gain_col_ref[...][None, :]
    for t in range(6):
        scratch[t] = normed[:, t * 128 : (t + 1) * 128]
    normed = jnp.concatenate(
        [
            jnp.concatenate([scratch[t, pl.ds(c, 64, stride=8), :] for c in range(8)], axis=0).astype(BF)
            for t in range(6)
        ],
        axis=1,
    )
    qkv[...] = mm(normed, attend[...]).astype(BF)
    group = lax.broadcasted_iota(jnp.int32, (256, 256), 0) // E == lax.broadcasted_iota(jnp.int32, (256, 256), 1) // E
    group = group.astype(F32).astype(BF)
    zeros = jnp.zeros((E, 256), BF)

    def tile(part, c, g):
        return qkv[c * 64 : (c + 1) * 64, part * 768 + g * 256 : part * 768 + (g + 1) * 256]

    def by_head(part, c, g):
        return jnp.concatenate([tile(part, c, g)] * 4, axis=0) * group

    for c in range(0, 8, 2):
        for g in range(3):
            k = jnp.concatenate([by_head(1, c, g), by_head(1, c + 1, g)], axis=1)
            q = jnp.concatenate(
                [
                    jnp.concatenate([tile(0, c, g), zeros], axis=1),
                    jnp.concatenate([zeros, tile(0, c + 1, g)], axis=1),
                ],
                axis=0,
            )
            scores = (mm_t(k, q) * (E ** -0.5)).reshape(4, 64, 128)
            expo = jnp.exp(scores - jnp.max(scores, axis=1, keepdims=True))
            weights = expo * (1.0 / jnp.sum(expo, axis=1, keepdims=True))
            weights = weights.reshape(256, 128).astype(BF)
            for k in range(2):
                mixed = lax.dot_general(
                    weights, by_head(2, c + k, g), (((0,), (0,)), ((), ())), preferred_element_type=F32
                )
                for t in range(2):
                    scratch[g * 2 + t, pl.ds(c + k, 64, stride=8), :] = mixed[
                        k * 64 : (k + 1) * 64, t * 128 : (t + 1) * 128
                    ]
    mixed = jnp.concatenate([scratch[t].astype(BF) for t in range(6)], axis=1)
    stream[...] += mm(mixed, exit_col[...])

    normed = normalize(stream[...], gain_ffn_ref[...][None, :])
    for copy in copies:
        copy.wait()
    for f in range(6):
        cols = slice(f * 512, (f + 1) * 512)
        pre = mm(normed, expand[:, cols])
        hidden = (0.5 * pre * (1.0 + lax.erf(pre * math.sqrt(0.5)))).astype(BF)
        stream[...] += mm(hidden, shrink[cols, :])
    done = stream[...].astype(BF)
    for i, (y, c, xl) in enumerate((y, c, xl) for y in range(4) for c in range(2) for xl in range(2)):
        out_ref[(xl * 4 + y) * 2 + c] = done[i * 32 : (i + 1) * 32, :]


def column_part(mix, x, gain_col, gain_ffn, exit_row, attend, exit_col, expand, shrink):
    vmem = pl.BlockSpec(memory_space=pltpu.VMEM)
    return pl.pallas_call(
        column_kernel,
        in_specs=[vmem] * 7 + [pl.BlockSpec(memory_space=pltpu.HBM)] * 2,
        out_specs=vmem,
        out_shape=jax.ShapeDtypeStruct((16, 32, 768), BF),
        scratch_shapes=[
            pltpu.VMEM((512, 2304), BF),
            pltpu.VMEM((512, 768), F32),
            pltpu.VMEM((6, 512, 128), F32),
            pltpu.VMEM(expand.shape, BF),
            pltpu.VMEM(shrink.shape, BF),
            pltpu.SemaphoreType.DMA((2,)),
        ],
        compiler_params=params(36),
        name="column_part",
    )(mix, x, gain_col, gain_ffn, exit_row, attend, exit_col, expand, shrink)


def local(
    embeddings,
    gain_row,
    attend_row,
    exit_row,
    gain_col,
    attend_col,
    exit_col,
    gain_ffn,
    expand,
    shrink,
):
    seq, col = lax.axis_index("seq"), lax.axis_index("col")
    core, y, z = seq % 2, seq // 2 % 4, col // 2
    place = jnp.stack([core, col % 2 * 2 + seq // 8, y, z]).astype(jnp.int32)
    scale = E ** (-0.5) / math.sqrt(embeddings.shape[0] * lax.axis_size("seq"))

    normed, *keys = key_proj(place, embeddings.reshape(512, 768), gain_row, attend_row)
    keys = over_x(keys)
    queries_values = query_value_proj(normed, attend_row)
    x = embeddings.reshape(4, 2, 8, 8, 768).transpose(2, 1, 0, 3, 4).reshape(16, 32, 768)
    keys, queries_values = lax.optimization_barrier((jnp.stack(keys), queries_values))

    keys0 = [keys] + [send(keys, dz=dz) for dz in (1, 3, 2)]
    keys1 = [to_other_core(k) for k in keys0]
    queries_values, x = lax.optimization_barrier((swap(queries_values, X_RINGS), x))
    x = lax.all_to_all(x, "seq", split_axis=0, concat_axis=0, tiled=True)
    queries, values = queries_values[:, 0], queries_values[:, 1]
    values = lax.optimization_barrier((values, x, keys1[0], *keys0))[0]
    values0 = gather(values, Z_RINGS)

    queries0 = lax.dynamic_slice_in_dim(queries, core * 64, 64, axis=3)
    queries1 = to_other_core(lax.dynamic_slice_in_dim(queries, (1 - core) * 64, 64, axis=3))
    scores = partial_scores(place, queries0, queries1, keys0, keys1)
    scores, x = lax.optimization_barrier((scores, x))
    weights = row_softmax(swap(scores, Y_RINGS), scale)
    weights, values0 = lax.optimization_barrier((weights, values0))
    weights = [weights] + [send(weights, dy=dy) for dy in (3, 2, 1)]
    mix = row_mix(place, weights, values0, to_other_core(values0))
    mix = swap(mix, PLANES).reshape(16, 3, 64, 128)

    out = column_part(mix, x, gain_col, gain_ffn, exit_row, attend_col, exit_col, expand, shrink)
    out = lax.all_to_all(out, "seq", split_axis=0, concat_axis=0, tiled=True)
    return out.reshape(8, 2, 4, 8, 768).transpose(2, 1, 0, 3, 4).reshape(4, 128, 768)


def solution(mesh):
    in_specs = (P("seq", "col", None), P(), P(), P(), P(), P(), P(), P(), P(), P())
    out_specs = P("seq", "col", None)
    return jax.shard_map(local, mesh=mesh, in_specs=in_specs, out_specs=out_specs, check_vma=False)
```

```python
import math

import jax
import jax.numpy as jnp
from jax import lax
from jax.experimental import pallas as pl
from jax.experimental.pallas import tpu as pltpu
from jax.sharding import PartitionSpec as P

AXES = ("seq", "col")
HEADS = 12
E = 64
BF = jnp.bfloat16
F32 = jnp.float32


def device(xl, y, c, z, xh):
    return ((xl * 4 + y) * 2 + c) * 8 + z * 2 + xh


R2, R4 = range(2), range(4)
Y_RINGS = [[device(xl, y, c, z, xh) for y in R4] for xl in R2 for c in R2 for z in R4 for xh in R2]
Z_COLUMNS = [[device(xl, y, c, z, xh) for z in R4 for c in R2] for xl in R2 for y in R4 for xh in R2]
X_RINGS = [[device(xl, y, c, z, xh) for xh in R2 for xl in R2] for y in R4 for c in R2 for z in R4]
PLANES = [[device(xl, y, c, z, xh) for xh in R2 for xl in R2 for y in R4] for c in R2 for z in R4]


def shifts(dx=0, dy=0, dz=0, dc=0):
    pairs = []
    for x in R4:
        for y in R4:
            for c in R2:
                for z in R4:
                    to = ((x + dx) % 4, (y + dy) % 4, (c + dc) % 2, (z + dz) % 4)
                    pairs.append((device(x % 2, y, c, z, x // 2), device(to[0] % 2, *to[1:], to[0] // 2)))
    return pairs


def params(mib):
    return pltpu.CompilerParams(vmem_limit_bytes=mib * 1024 * 1024)


def swap(array, groups):
    return lax.all_to_all(array, AXES, split_axis=0, concat_axis=0, tiled=True, axis_index_groups=groups)


def gather(array, groups):
    return lax.all_gather(array, AXES, axis=0, tiled=False, axis_index_groups=groups)


def send(array, **by):
    return lax.ppermute(array, AXES, shifts(**by))


def to_other_core(array):
    return send(array, dc=1)


def mm(a, b):
    return jnp.dot(a, b, preferred_element_type=F32)


def mm_t(a, b):
    return lax.dot_general(a, b, (((1,), (1,)), ((), ())), preferred_element_type=F32)


def centre(stream):
    mean = jnp.mean(stream, axis=-1, keepdims=True)
    centred = stream - mean
    var = jnp.mean(centred * centred, axis=-1, keepdims=True)
    return centred * lax.rsqrt(var + 1e-05)


def normalize(stream, gain):
    return (centre(stream) * gain).astype(BF)


CORE, X, Y, Z = range(4)
SCALARS = pl.BlockSpec(memory_space=pltpu.SMEM)


def write_pairs(normed, weight, out):
    low = lax.broadcasted_iota(jnp.int32, (128, 128), 1) < E
    for rp in range(2):
        first = mm(normed[2 * rp * 128 : (2 * rp + 1) * 128, :], weight)
        second = mm(normed[(2 * rp + 1) * 128 : (2 * rp + 2) * 128, :], weight)
        for t in range(6):
            a, b = first[:, t * 128 : (t + 1) * 128], second[:, t * 128 : (t + 1) * 128]
            pair = (
                jnp.where(low, a, pltpu.roll(b, E, 1)),
                jnp.where(low, pltpu.roll(a, E, 1), b),
            )
            for k in range(2):
                g, h = (2 * t + k) // 3, (2 * t + k) % 3
                out[g, h, rp] = pair[k].astype(BF)


def key_kernel(place_ref, x_ref, gain_ref, w_ref, normed_ref, *refs):
    normed_ref[...] = normalize(x_ref[...].astype(F32), gain_ref[...][None, :])
    outs, pieces = refs[:4], refs[4]
    write_pairs(normed_ref[...], w_ref[...], pieces)
    for s, out in enumerate(outs):
        out[...] = pieces[(place_ref[X] + s) % 4]


def key_proj(place, x, gain, weight):
    piece = (3, 2, 128, 128)
    return pl.pallas_call(
        key_kernel,
        grid=(1,),
        in_specs=[
            SCALARS,
            pl.BlockSpec((512, 768), lambda i: (0, 0)),
            pl.BlockSpec((768,), lambda i: (0,)),
            pl.BlockSpec((768, 768), lambda i: (0, 1)),
        ],
        out_specs=[pl.BlockSpec((512, 768), lambda i: (0, 0))] + [pl.BlockSpec(piece, lambda i: (0, 0, 0, 0))] * 4,
        out_shape=[jax.ShapeDtypeStruct((512, 768), BF)] + [jax.ShapeDtypeStruct(piece, BF)] * 4,
        scratch_shapes=[pltpu.VMEM((4,) + piece, BF)],
        compiler_params=params(56),
        name="key_proj",
    )(place, x, gain, weight)


def query_value_kernel(normed_ref, w_ref, out_ref):
    write_pairs(normed_ref[...], w_ref[...], out_ref.at[:, 0])


def query_value_proj(normed, weight):
    return pl.pallas_call(
        query_value_kernel,
        grid=(2,),
        in_specs=[
            pl.BlockSpec((512, 768), lambda i: (0, 0)),
            pl.BlockSpec((768, 768), lambda i: (0, 2 * i)),
        ],
        out_specs=pl.BlockSpec((4, 1, 3, 2, 128, 128), lambda i: (0, i, 0, 0, 0, 0)),
        out_shape=jax.ShapeDtypeStruct((4, 2, 3, 2, 128, 128), BF),
        compiler_params=params(16),
        name="query_value_proj",
    )(normed, weight)


def over_x(pieces):
    return [pieces[0], send(pieces[3], dx=3), send(pieces[2], dx=2), send(pieces[1], dx=1)]


def scores_kernel(place_ref, q0_ref, q1_ref, keys_hbm, out_ref, keys, sems):
    copies = [
        pltpu.make_async_copy(keys_hbm.at[z * 2 : z * 2 + 2], keys.at[z * 2 : z * 2 + 2], sems.at[z]) for z in range(4)
    ]
    for copy in copies:
        copy.start()
    left = [
        jnp.concatenate(
            [
                jnp.concatenate(
                    [
                        q[xh * 2 + xl, h, rp]
                        for q in (q0_ref, q1_ref)
                        for xl in range(2)
                        for rp in range(2)
                    ],
                    axis=1,
                )
                for xh in range(2)
            ],
            axis=0,
        )
        for h in range(3)
    ]
    for z in range(4):
        copies[z].wait()
        for h in range(3):
            right = [
                jnp.concatenate(
                    [
                        keys[z * 2 + (place_ref[CORE] + k) % 2, (xh * 2 + xl + 4 - place_ref[X]) % 4, h, rp]
                        for k in range(2)
                        for xl in range(2)
                        for rp in range(2)
                    ],
                    axis=1,
                )
                for xh in range(2)
            ]
            scores = mm_t(left[h], jnp.concatenate(right, axis=0))
            out_ref[:, h, :, z * 256 : (z + 1) * 256] = scores.reshape(4, 32, 256)


def partial_scores(place, q0, q1, keys):
    vmem = pl.BlockSpec(memory_space=pltpu.VMEM)
    return pl.pallas_call(
        scores_kernel,
        in_specs=[SCALARS, vmem, vmem, pl.BlockSpec(memory_space=pltpu.HBM)],
        out_specs=vmem,
        out_shape=jax.ShapeDtypeStruct((4, 3, 32, 1024), F32),
        scratch_shapes=[pltpu.VMEM(keys.shape, BF), pltpu.SemaphoreType.DMA((4,))],
        compiler_params=params(56),
        name="partial_scores",
    )(place, q0, q1, keys)


def softmax_kernel(scale, parts_ref, out_ref):
    tied = (parts_ref[0] + parts_ref[1] + parts_ref[2] + parts_ref[3]) * scale
    expo = jnp.exp(tied - jnp.max(tied, axis=-1, keepdims=True))
    out_ref[...] = (expo / jnp.sum(expo, axis=-1, keepdims=True)).astype(BF)


def row_softmax(parts, scale):
    return pl.pallas_call(
        lambda *refs: softmax_kernel(scale, *refs),
        in_specs=[pl.BlockSpec(memory_space=pltpu.VMEM)],
        out_specs=pl.BlockSpec(memory_space=pltpu.VMEM),
        out_shape=jax.ShapeDtypeStruct((3, 32, 1024), BF),
        compiler_params=params(8),
        name="row_softmax",
    )(parts)


def mix_kernel(place_ref, w0_ref, w1_ref, w2_ref, w3_ref, values_hbm, out_ref, weights, values, sems):
    order = [(c, xl) for c in range(2) for xl in range(2)]
    copies = [
        pltpu.make_async_copy(values_hbm.at[z * 2 + c, xh * 2 + xl], values.at[z * 2 + c, xh * 2 + xl], sems.at[i, z, xh])
        for i, (c, xl) in enumerate(order)
        for z in range(4)
        for xh in range(2)
    ]
    for copy in copies:
        copy.start()
    for d, w in enumerate((w0_ref, w1_ref, w2_ref, w3_ref)):
        share = (place_ref[Y] + d) % 4
        weights[:, pl.ds(pl.multiple_of(share * 32, 32), 32), :] = w[...]
    for i, (c, xl) in enumerate(order):
        for copy in copies[i * 8 : i * 8 + 8]:
            copy.wait()
        for h in range(3):
            right = [
                jnp.concatenate([values[z * 2 + c, xh * 2 + xl, h, rp] for rp in range(2)], axis=1)
                for z in range(4)
                for xh in range(2)
            ]
            mixed = mm(weights[h], jnp.concatenate(right, axis=0))
            pair = jnp.concatenate(
                [mixed[:, :128].reshape(16, 8, 128), mixed[:, 128:].reshape(16, 8, 128)], axis=1
            )
            out_ref[:, h, c, xl * 16 : (xl + 1) * 16, :] = pair.astype(BF)


def row_mix(place, weights, values):
    vmem = pl.BlockSpec(memory_space=pltpu.VMEM)
    return pl.pallas_call(
        mix_kernel,
        in_specs=[SCALARS] + [vmem] * 4 + [pl.BlockSpec(memory_space=pltpu.HBM)],
        out_specs=vmem,
        out_shape=jax.ShapeDtypeStruct((16, 3, 2, 32, 128), BF),
        scratch_shapes=[
            pltpu.VMEM((3, 128, 1024), BF),
            pltpu.VMEM(values.shape, BF),
            pltpu.SemaphoreType.DMA((4, 4, 2)),
        ],
        compiler_params=params(58),
        name="row_mix",
    )(place, *weights, values)


def column_kernel(
    mix_ref, x_ref, gain_col_ref, gain_ffn_ref, exit_row, attend, exit_col, expand_hbm, shrink_hbm,
    out_ref, qkv, stream, scratch, expand, shrink, sems,
):
    copies = [
        pltpu.make_async_copy(expand_hbm, expand, sems.at[0]),
        pltpu.make_async_copy(shrink_hbm, shrink, sems.at[1]),
    ]
    for copy in copies:
        copy.start()
    low = lax.broadcasted_iota(jnp.int32, (64, 128), 1) < E
    halves = ([], [])
    for y in range(4):
        tiles = ([], [])
        for t in range(6):
            (g0, h0), (g1, h1) = divmod(2 * t, 3), divmod(2 * t + 1, 3)
            a = mix_ref[g0 * 4 + y, h0].astype(F32)
            b = mix_ref[g1 * 4 + y, h1].astype(F32)
            tiles[0].append(jnp.where(low, a, pltpu.roll(b, E, 1)).astype(BF))
            tiles[1].append(jnp.where(low, pltpu.roll(a, E, 1), b).astype(BF))
        for k in range(2):
            halves[k].append(jnp.concatenate(tiles[k], axis=1))
    exits = [mm(jnp.concatenate(halves[k], axis=0), exit_row[...]).reshape(32, 1, 8, 768) for k in range(2)]
    exits = jnp.concatenate(exits, axis=1).reshape(512, 768)
    x = jnp.concatenate([x_ref[(xl * 4 + y) * 2 + c] for y in range(4) for c in range(2) for xl in range(2)], axis=0)
    stream[...] = x.astype(F32) + exits

    normed = centre(stream[...]) * gain_col_ref[...][None, :]
    for t in range(6):
        scratch[t] = normed[:, t * 128 : (t + 1) * 128]
    normed = jnp.concatenate(
        [
            jnp.concatenate([scratch[t, pl.ds(c, 64, stride=8), :] for c in range(8)], axis=0).astype(BF)
            for t in range(6)
        ],
        axis=1,
    )
    qkv[...] = mm(normed, attend[...]).astype(BF)
    group = lax.broadcasted_iota(jnp.int32, (256, 256), 0) // E == lax.broadcasted_iota(jnp.int32, (256, 256), 1) // E
    group = group.astype(F32).astype(BF)
    zeros = jnp.zeros((E, 256), BF)

    def tile(part, c, g):
        return qkv[c * 64 : (c + 1) * 64, part * 768 + g * 256 : part * 768 + (g + 1) * 256]

    def by_head(part, c, g):
        return jnp.concatenate([tile(part, c, g)] * 4, axis=0) * group

    for c in range(0, 8, 2):
        for g in range(3):
            k = jnp.concatenate([by_head(1, c, g), by_head(1, c + 1, g)], axis=1)
            q = jnp.concatenate(
                [
                    jnp.concatenate([tile(0, c, g), zeros], axis=1),
                    jnp.concatenate([zeros, tile(0, c + 1, g)], axis=1),
                ],
                axis=0,
            )
            scores = (mm_t(k, q) * (E ** -0.5)).reshape(4, 64, 128)
            expo = jnp.exp(scores - jnp.max(scores, axis=1, keepdims=True))
            weights = expo * (1.0 / jnp.sum(expo, axis=1, keepdims=True))
            weights = weights.reshape(256, 128).astype(BF)
            for k in range(2):
                mixed = lax.dot_general(
                    weights, by_head(2, c + k, g), (((0,), (0,)), ((), ())), preferred_element_type=F32
                )
                for t in range(2):
                    scratch[g * 2 + t, pl.ds(c + k, 64, stride=8), :] = mixed[
                        k * 64 : (k + 1) * 64, t * 128 : (t + 1) * 128
                    ]
    mixed = jnp.concatenate([scratch[t].astype(BF) for t in range(6)], axis=1)
    stream[...] += mm(mixed, exit_col[...])

    normed = normalize(stream[...], gain_ffn_ref[...][None, :])
    for copy in copies:
        copy.wait()
    for f in range(6):
        cols = slice(f * 512, (f + 1) * 512)
        pre = mm(normed, expand[:, cols])
        hidden = (0.5 * pre * (1.0 + lax.erf(pre * math.sqrt(0.5)))).astype(BF)
        stream[...] += mm(hidden, shrink[cols, :])
    done = stream[...].astype(BF)
    for i, (y, c, xl) in enumerate((y, c, xl) for y in range(4) for c in range(2) for xl in range(2)):
        out_ref[(xl * 4 + y) * 2 + c] = done[i * 32 : (i + 1) * 32, :]


def column_part(mix, x, gain_col, gain_ffn, exit_row, attend, exit_col, expand, shrink):
    vmem = pl.BlockSpec(memory_space=pltpu.VMEM)
    return pl.pallas_call(
        column_kernel,
        in_specs=[vmem] * 7 + [pl.BlockSpec(memory_space=pltpu.HBM)] * 2,
        out_specs=vmem,
        out_shape=jax.ShapeDtypeStruct((16, 32, 768), BF),
        scratch_shapes=[
            pltpu.VMEM((512, 2304), BF),
            pltpu.VMEM((512, 768), F32),
            pltpu.VMEM((6, 512, 128), F32),
            pltpu.VMEM(expand.shape, BF),
            pltpu.VMEM(shrink.shape, BF),
            pltpu.SemaphoreType.DMA((2,)),
        ],
        compiler_params=params(48),
        name="column_part",
    )(mix, x, gain_col, gain_ffn, exit_row, attend, exit_col, expand, shrink)


def local(
    embeddings,
    gain_row,
    attend_row,
    exit_row,
    gain_col,
    attend_col,
    exit_col,
    gain_ffn,
    expand,
    shrink,
):
    seq, col = lax.axis_index("seq"), lax.axis_index("col")
    core, y, z = seq % 2, seq // 2 % 4, col // 2
    place = jnp.stack([core, col % 2 * 2 + seq // 8, y, z]).astype(jnp.int32)
    scale = E ** (-0.5) / math.sqrt(embeddings.shape[0] * lax.axis_size("seq"))

    normed, *keys = key_proj(place, embeddings.reshape(512, 768), gain_row, attend_row)
    keys = over_x(keys)
    queries_values = query_value_proj(normed, attend_row)
    x = embeddings.reshape(4, 2, 8, 8, 768).transpose(2, 1, 0, 3, 4).reshape(16, 32, 768)
    keys, queries_values = lax.optimization_barrier((jnp.stack(keys), queries_values))

    keys_all = gather(keys, Z_COLUMNS)
    queries_values, x = lax.optimization_barrier((swap(queries_values, X_RINGS), x))
    x = lax.all_to_all(x, "seq", split_axis=0, concat_axis=0, tiled=True)
    queries, values = queries_values[:, 0], queries_values[:, 1]
    values = lax.optimization_barrier((values, keys))[0]
    values = gather(values, Z_COLUMNS)

    queries0 = lax.dynamic_slice_in_dim(queries, core * 64, 64, axis=3)
    queries1 = to_other_core(lax.dynamic_slice_in_dim(queries, (1 - core) * 64, 64, axis=3))
    keys = lax.optimization_barrier((keys_all, x, queries1))[0]
    scores = partial_scores(place, queries0, queries1, keys)
    scores, x = lax.optimization_barrier((scores, x))
    weights = row_softmax(swap(scores, Y_RINGS), scale)
    values = lax.optimization_barrier((values, weights))[0]
    weights = [weights] + [send(weights, dy=dy) for dy in (3, 2, 1)]
    mix = row_mix(place, weights, values)
    mix = swap(mix, PLANES).reshape(16, 3, 64, 128)

    out = column_part(mix, x, gain_col, gain_ffn, exit_row, attend_col, exit_col, expand, shrink)
    out = lax.all_to_all(out, "seq", split_axis=0, concat_axis=0, tiled=True)
    return out.reshape(8, 2, 4, 8, 768).transpose(2, 1, 0, 3, 4).reshape(4, 128, 768)


def solution(mesh):
    in_specs = (P("seq", "col", None), P(), P(), P(), P(), P(), P(), P(), P(), P())
    out_specs = P("seq", "col", None)
    return jax.shard_map(local, mesh=mesh, in_specs=in_specs, out_specs=out_specs, check_vma=False)
```

```python
import math

import jax
import jax.numpy as jnp
from jax import lax
from jax.experimental import pallas as pl
from jax.experimental.pallas import tpu as pltpu
from jax.sharding import PartitionSpec as P

AXES = ("seq", "col")
HEADS = 12
E = 64
BF = jnp.bfloat16
F32 = jnp.float32


def device(xl, y, c, z, xh):
    return ((xl * 4 + y) * 2 + c) * 8 + z * 2 + xh


R2, R4 = range(2), range(4)
Y_RINGS = [[device(xl, y, c, z, xh) for y in R4] for xl in R2 for c in R2 for z in R4 for xh in R2]
Z_COLUMNS = [[device(xl, y, c, z, xh) for z in R4 for c in R2] for xl in R2 for y in R4 for xh in R2]
X_RINGS = [[device(xl, y, c, z, xh) for xh in R2 for xl in R2] for y in R4 for c in R2 for z in R4]
PLANES = [[device(xl, y, c, z, xh) for xh in R2 for xl in R2 for y in R4] for c in R2 for z in R4]


def shifts(dx=0, dy=0, dz=0, dc=0):
    pairs = []
    for x in R4:
        for y in R4:
            for c in R2:
                for z in R4:
                    to = ((x + dx) % 4, (y + dy) % 4, (c + dc) % 2, (z + dz) % 4)
                    pairs.append((device(x % 2, y, c, z, x // 2), device(to[0] % 2, *to[1:], to[0] // 2)))
    return pairs


def params(mib):
    return pltpu.CompilerParams(vmem_limit_bytes=mib * 1024 * 1024)


def swap(array, groups):
    return lax.all_to_all(array, AXES, split_axis=0, concat_axis=0, tiled=True, axis_index_groups=groups)


def gather(array, groups):
    return lax.all_gather(array, AXES, axis=0, tiled=False, axis_index_groups=groups)


def send(array, **by):
    return lax.ppermute(array, AXES, shifts(**by))


def to_other_core(array):
    return send(array, dc=1)


def mm(a, b):
    return jnp.dot(a, b, preferred_element_type=F32)


def mm_t(a, b):
    return lax.dot_general(a, b, (((1,), (1,)), ((), ())), preferred_element_type=F32)


def centre(stream):
    mean = jnp.mean(stream, axis=-1, keepdims=True)
    centred = stream - mean
    var = jnp.mean(centred * centred, axis=-1, keepdims=True)
    return centred * lax.rsqrt(var + 1e-05)


def normalize(stream, gain):
    return (centre(stream) * gain).astype(BF)


CORE, X, Y, Z = range(4)
SCALARS = pl.BlockSpec(memory_space=pltpu.SMEM)


def write_pairs(normed, weight, out):
    low = lax.broadcasted_iota(jnp.int32, (128, 128), 1) < E
    first, second = mm(normed[:128, :], weight), mm(normed[128:, :], weight)
    for t in range(6):
        a, b = first[:, t * 128 : (t + 1) * 128], second[:, t * 128 : (t + 1) * 128]
        pair = (
            jnp.where(low, a, pltpu.roll(b, E, 1)),
            jnp.where(low, pltpu.roll(a, E, 1), b),
        )
        for k in range(2):
            g, h = (2 * t + k) // 3, (2 * t + k) % 3
            out[g, h] = pair[k].astype(BF)


def key_kernel(place_ref, x_ref, gain_ref, w_ref, normed_ref, *refs):
    normed_ref[...] = normalize(x_ref[...].astype(F32), gain_ref[...][None, :])
    outs, pieces = refs[:4], refs[4]
    write_pairs(normed_ref[...], w_ref[...], pieces)
    for s, out in enumerate(outs):
        out[:, 0] = pieces[(place_ref[X] + s) % 4]


def key_proj(place, x, gain, weight):
    piece = (3, 2, 128, 128)
    return pl.pallas_call(
        key_kernel,
        grid=(2,),
        in_specs=[
            SCALARS,
            pl.BlockSpec((256, 768), lambda i: (i, 0)),
            pl.BlockSpec((768,), lambda i: (0,)),
            pl.BlockSpec((768, 768), lambda i: (0, 1)),
        ],
        out_specs=[pl.BlockSpec((256, 768), lambda i: (i, 0))]
        + [pl.BlockSpec((3, 1, 128, 128), lambda i: (0, i, 0, 0))] * 4,
        out_shape=[jax.ShapeDtypeStruct((512, 768), BF)] + [jax.ShapeDtypeStruct(piece, BF)] * 4,
        scratch_shapes=[pltpu.VMEM((4, 3, 128, 128), BF)],
        compiler_params=params(52),
        name="key_proj",
    )(place, x, gain, weight)


def query_value_kernel(normed_ref, w_ref, out_ref):
    for rp in range(2):
        write_pairs(normed_ref[rp * 256 : (rp + 1) * 256, :], w_ref[...], out_ref.at[:, 0, :, rp])


def query_value_proj(normed, weight):
    return pl.pallas_call(
        query_value_kernel,
        grid=(2,),
        in_specs=[
            pl.BlockSpec((512, 768), lambda i: (0, 0)),
            pl.BlockSpec((768, 768), lambda i: (0, 2 * i)),
        ],
        out_specs=pl.BlockSpec((4, 1, 3, 2, 128, 128), lambda i: (0, i, 0, 0, 0, 0)),
        out_shape=jax.ShapeDtypeStruct((4, 2, 3, 2, 128, 128), BF),
        compiler_params=params(16),
        name="query_value_proj",
    )(normed, weight)


def over_x(pieces):
    return [pieces[0], send(pieces[3], dx=3), send(pieces[2], dx=2), send(pieces[1], dx=1)]


def scores_kernel(place_ref, q0_ref, q1_ref, keys_hbm, out_ref, keys, sems):
    copies = [
        pltpu.make_async_copy(keys_hbm.at[z * 2 : z * 2 + 2], keys.at[z * 2 : z * 2 + 2], sems.at[z]) for z in range(4)
    ]
    for copy in copies:
        copy.start()
    left = [
        jnp.concatenate(
            [
                jnp.concatenate(
                    [
                        q[xh * 2 + xl, h, rp]
                        for q in (q0_ref, q1_ref)
                        for xl in range(2)
                        for rp in range(2)
                    ],
                    axis=1,
                )
                for xh in range(2)
            ],
            axis=0,
        )
        for h in range(3)
    ]
    for z in range(4):
        copies[z].wait()
        for h in range(3):
            right = [
                jnp.concatenate(
                    [
                        keys[z * 2 + (place_ref[CORE] + k) % 2, (xh * 2 + xl + 4 - place_ref[X]) % 4, h, rp]
                        for k in range(2)
                        for xl in range(2)
                        for rp in range(2)
                    ],
                    axis=1,
                )
                for xh in range(2)
            ]
            scores = mm_t(left[h], jnp.concatenate(right, axis=0))
            out_ref[:, h, :, z * 256 : (z + 1) * 256] = scores.reshape(4, 32, 256)


def partial_scores(place, q0, q1, keys):
    vmem = pl.BlockSpec(memory_space=pltpu.VMEM)
    return pl.pallas_call(
        scores_kernel,
        in_specs=[SCALARS, vmem, vmem, pl.BlockSpec(memory_space=pltpu.HBM)],
        out_specs=vmem,
        out_shape=jax.ShapeDtypeStruct((4, 3, 32, 1024), F32),
        scratch_shapes=[pltpu.VMEM(keys.shape, BF), pltpu.SemaphoreType.DMA((4,))],
        compiler_params=params(48),
        name="partial_scores",
    )(place, q0, q1, keys)


def softmax_kernel(scale, parts_ref, out_ref):
    tied = (parts_ref[0] + parts_ref[1] + parts_ref[2] + parts_ref[3]) * scale
    expo = jnp.exp(tied - jnp.max(tied, axis=-1, keepdims=True))
    out_ref[...] = (expo / jnp.sum(expo, axis=-1, keepdims=True)).astype(BF)


def row_softmax(parts, scale):
    return pl.pallas_call(
        lambda *refs: softmax_kernel(scale, *refs),
        in_specs=[pl.BlockSpec(memory_space=pltpu.VMEM)],
        out_specs=pl.BlockSpec(memory_space=pltpu.VMEM),
        out_shape=jax.ShapeDtypeStruct((3, 32, 1024), BF),
        compiler_params=params(8),
        name="row_softmax",
    )(parts)


def mix_kernel(place_ref, w0_ref, w1_ref, w2_ref, w3_ref, values, out_ref, weights):
    for d, w in enumerate((w0_ref, w1_ref, w2_ref, w3_ref)):
        share = (place_ref[Y] + d) % 4
        weights[:, pl.ds(pl.multiple_of(share * 32, 32), 32), :] = w[...]
    for c in range(2):
        for xl in range(2):
            for h in range(3):
                right = [
                    jnp.concatenate([values[z * 2 + c, xh * 2 + xl, h, rp] for rp in range(2)], axis=1)
                    for z in range(4)
                    for xh in range(2)
                ]
                mixed = mm(weights[h], jnp.concatenate(right, axis=0))
                pair = jnp.concatenate(
                    [mixed[:, :128].reshape(16, 8, 128), mixed[:, 128:].reshape(16, 8, 128)], axis=1
                )
                out_ref[:, h, c, xl * 16 : (xl + 1) * 16, :] = pair.astype(BF)


def row_mix(place, weights, values):
    vmem = pl.BlockSpec(memory_space=pltpu.VMEM)
    return pl.pallas_call(
        mix_kernel,
        in_specs=[SCALARS] + [vmem] * 5,
        out_specs=vmem,
        out_shape=jax.ShapeDtypeStruct((16, 3, 2, 32, 128), BF),
        scratch_shapes=[pltpu.VMEM((3, 128, 1024), BF)],
        compiler_params=params(14),
        name="row_mix",
    )(place, *weights, values)


def column_kernel(
    mix_ref, x_ref, gain_col_ref, gain_ffn_ref, exit_row, attend, exit_col, expand_hbm, shrink_hbm,
    out_ref, qkv, stream, scratch, expand, shrink, sems,
):
    copies = [
        pltpu.make_async_copy(expand_hbm, expand, sems.at[0]),
        pltpu.make_async_copy(shrink_hbm, shrink, sems.at[1]),
    ]
    for copy in copies:
        copy.start()
    low = lax.broadcasted_iota(jnp.int32, (64, 128), 1) < E
    halves = ([], [])
    for y in range(4):
        tiles = ([], [])
        for t in range(6):
            (g0, h0), (g1, h1) = divmod(2 * t, 3), divmod(2 * t + 1, 3)
            a = mix_ref[g0 * 4 + y, h0].astype(F32)
            b = mix_ref[g1 * 4 + y, h1].astype(F32)
            tiles[0].append(jnp.where(low, a, pltpu.roll(b, E, 1)).astype(BF))
            tiles[1].append(jnp.where(low, pltpu.roll(a, E, 1), b).astype(BF))
        for k in range(2):
            halves[k].append(jnp.concatenate(tiles[k], axis=1))
    exits = [mm(jnp.concatenate(halves[k], axis=0), exit_row[...]).reshape(32, 1, 8, 768) for k in range(2)]
    exits = jnp.concatenate(exits, axis=1).reshape(512, 768)
    x = jnp.concatenate([x_ref[(xl * 4 + y) * 2 + c] for y in range(4) for c in range(2) for xl in range(2)], axis=0)
    stream[...] = x.astype(F32) + exits

    normed = centre(stream[...]) * gain_col_ref[...][None, :]
    for t in range(6):
        scratch[t] = normed[:, t * 128 : (t + 1) * 128]
    normed = jnp.concatenate(
        [
            jnp.concatenate([scratch[t, pl.ds(c, 64, stride=8), :] for c in range(8)], axis=0).astype(BF)
            for t in range(6)
        ],
        axis=1,
    )
    qkv[...] = mm(normed, attend[...]).astype(BF)
    group = lax.broadcasted_iota(jnp.int32, (256, 256), 0) // E == lax.broadcasted_iota(jnp.int32, (256, 256), 1) // E
    group = group.astype(F32).astype(BF)
    zeros = jnp.zeros((E, 256), BF)

    def tile(part, c, g):
        return qkv[c * 64 : (c + 1) * 64, part * 768 + g * 256 : part * 768 + (g + 1) * 256]

    def by_head(part, c, g):
        return jnp.concatenate([tile(part, c, g)] * 4, axis=0) * group

    for c in range(0, 8, 2):
        for g in range(3):
            k = jnp.concatenate([by_head(1, c, g), by_head(1, c + 1, g)], axis=1)
            q = jnp.concatenate(
                [
                    jnp.concatenate([tile(0, c, g), zeros], axis=1),
                    jnp.concatenate([zeros, tile(0, c + 1, g)], axis=1),
                ],
                axis=0,
            )
            scores = (mm_t(k, q) * (E ** -0.5)).reshape(4, 64, 128)
            expo = jnp.exp(scores - jnp.max(scores, axis=1, keepdims=True))
            weights = expo * (1.0 / jnp.sum(expo, axis=1, keepdims=True))
            weights = weights.reshape(256, 128).astype(BF)
            for k in range(2):
                mixed = lax.dot_general(
                    weights, by_head(2, c + k, g), (((0,), (0,)), ((), ())), preferred_element_type=F32
                )
                for t in range(2):
                    scratch[g * 2 + t, pl.ds(c + k, 64, stride=8), :] = mixed[
                        k * 64 : (k + 1) * 64, t * 128 : (t + 1) * 128
                    ]
    mixed = jnp.concatenate([scratch[t].astype(BF) for t in range(6)], axis=1)
    stream[...] += mm(mixed, exit_col[...])

    normed = normalize(stream[...], gain_ffn_ref[...][None, :])
    for copy in copies:
        copy.wait()
    for f in range(6):
        cols = slice(f * 512, (f + 1) * 512)
        pre = mm(normed, expand[:, cols])
        hidden = (0.5 * pre * (1.0 + lax.erf(pre * math.sqrt(0.5)))).astype(BF)
        stream[...] += mm(hidden, shrink[cols, :])
    done = stream[...].astype(BF)
    for i, (y, c, xl) in enumerate((y, c, xl) for y in range(4) for c in range(2) for xl in range(2)):
        out_ref[(xl * 4 + y) * 2 + c] = done[i * 32 : (i + 1) * 32, :]


def column_part(mix, x, gain_col, gain_ffn, exit_row, attend, exit_col, expand, shrink):
    vmem = pl.BlockSpec(memory_space=pltpu.VMEM)
    return pl.pallas_call(
        column_kernel,
        in_specs=[vmem] * 7 + [pl.BlockSpec(memory_space=pltpu.HBM)] * 2,
        out_specs=vmem,
        out_shape=jax.ShapeDtypeStruct((16, 32, 768), BF),
        scratch_shapes=[
            pltpu.VMEM((512, 2304), BF),
            pltpu.VMEM((512, 768), F32),
            pltpu.VMEM((6, 512, 128), F32),
            pltpu.VMEM(expand.shape, BF),
            pltpu.VMEM(shrink.shape, BF),
            pltpu.SemaphoreType.DMA((2,)),
        ],
        compiler_params=params(48),
        name="column_part",
    )(mix, x, gain_col, gain_ffn, exit_row, attend, exit_col, expand, shrink)


def local(
    embeddings,
    gain_row,
    attend_row,
    exit_row,
    gain_col,
    attend_col,
    exit_col,
    gain_ffn,
    expand,
    shrink,
):
    seq, col = lax.axis_index("seq"), lax.axis_index("col")
    core, y, z = seq % 2, seq // 2 % 4, col // 2
    place = jnp.stack([core, col % 2 * 2 + seq // 8, y, z]).astype(jnp.int32)
    scale = E ** (-0.5) / math.sqrt(embeddings.shape[0] * lax.axis_size("seq"))

    normed, *keys = key_proj(place, embeddings.reshape(512, 768), gain_row, attend_row)
    keys = over_x(keys)
    queries_values = query_value_proj(normed, attend_row)
    x = embeddings.reshape(4, 2, 8, 8, 768).transpose(2, 1, 0, 3, 4).reshape(16, 32, 768)
    keys, queries_values = lax.optimization_barrier((jnp.stack(keys), queries_values))

    keys_all = gather(keys, Z_COLUMNS)
    queries_values, x = lax.optimization_barrier((swap(queries_values, X_RINGS), x))
    x = lax.all_to_all(x, "seq", split_axis=0, concat_axis=0, tiled=True)
    queries, values = queries_values[:, 0], queries_values[:, 1]
    values = lax.optimization_barrier((values, keys))[0]
    values = gather(values, Z_COLUMNS)

    queries0 = lax.dynamic_slice_in_dim(queries, core * 64, 64, axis=3)
    queries1 = to_other_core(lax.dynamic_slice_in_dim(queries, (1 - core) * 64, 64, axis=3))
    keys = lax.optimization_barrier((keys_all, x, queries1))[0]
    scores = partial_scores(place, queries0, queries1, keys)
    scores, x = lax.optimization_barrier((scores, x))
    weights = row_softmax(swap(scores, Y_RINGS), scale)
    values = lax.optimization_barrier((values, weights))[0]
    weights = [weights] + [send(weights, dy=dy) for dy in (3, 2, 1)]
    mix = row_mix(place, weights, values)
    mix = swap(mix, PLANES).reshape(16, 3, 64, 128)

    out = column_part(mix, x, gain_col, gain_ffn, exit_row, attend_col, exit_col, expand, shrink)
    out = lax.all_to_all(out, "seq", split_axis=0, concat_axis=0, tiled=True)
    return out.reshape(8, 2, 4, 8, 768).transpose(2, 1, 0, 3, 4).reshape(4, 128, 768)


def solution(mesh):
    in_specs = (P("seq", "col", None), P(), P(), P(), P(), P(), P(), P(), P(), P())
    out_specs = P("seq", "col", None)
    return jax.shard_map(local, mesh=mesh, in_specs=in_specs, out_specs=out_specs, check_vma=False)
```

```python
import math

import jax
import jax.numpy as jnp
from jax import lax
from jax.experimental import pallas as pl
from jax.experimental.pallas import tpu as pltpu
from jax.sharding import PartitionSpec as P

AXES = ("seq", "col")
HEADS = 12
E = 64
BF = jnp.bfloat16
F32 = jnp.float32


def device(xl, y, c, z, xh):
    return ((xl * 4 + y) * 2 + c) * 8 + z * 2 + xh


R2, R4 = range(2), range(4)
Y_RINGS = [[device(xl, y, c, z, xh) for y in R4] for xl in R2 for c in R2 for z in R4 for xh in R2]
Z_COLUMNS = [[device(xl, y, c, z, xh) for z in R4 for c in R2] for xl in R2 for y in R4 for xh in R2]
X_RINGS = [[device(xl, y, c, z, xh) for xh in R2 for xl in R2] for y in R4 for c in R2 for z in R4]
PLANES = [[device(xl, y, c, z, xh) for xh in R2 for xl in R2 for y in R4] for c in R2 for z in R4]


def shifts(dx=0, dy=0, dz=0, dc=0):
    pairs = []
    for x in R4:
        for y in R4:
            for c in R2:
                for z in R4:
                    to = ((x + dx) % 4, (y + dy) % 4, (c + dc) % 2, (z + dz) % 4)
                    pairs.append((device(x % 2, y, c, z, x // 2), device(to[0] % 2, *to[1:], to[0] // 2)))
    return pairs


def params(mib):
    return pltpu.CompilerParams(vmem_limit_bytes=mib * 1024 * 1024)


def swap(array, groups):
    return lax.all_to_all(array, AXES, split_axis=0, concat_axis=0, tiled=True, axis_index_groups=groups)


def gather(array, groups):
    return lax.all_gather(array, AXES, axis=0, tiled=False, axis_index_groups=groups)


def send(array, **by):
    return lax.ppermute(array, AXES, shifts(**by))


def to_other_core(array):
    return send(array, dc=1)


def mm(a, b):
    return jnp.dot(a, b, preferred_element_type=F32)


def mm_t(a, b):
    return lax.dot_general(a, b, (((1,), (1,)), ((), ())), preferred_element_type=F32)


def centre(stream):
    mean = jnp.mean(stream, axis=-1, keepdims=True)
    centred = stream - mean
    var = jnp.mean(centred * centred, axis=-1, keepdims=True)
    return centred * lax.rsqrt(var + 1e-05)


def normalize(stream, gain):
    return (centre(stream) * gain).astype(BF)


CORE, X, Y, Z = range(4)
SCALARS = pl.BlockSpec(memory_space=pltpu.SMEM)


def write_pairs(normed, weight, out):
    low = lax.broadcasted_iota(jnp.int32, (128, 128), 1) < E
    first, second = mm(normed[:128, :], weight), mm(normed[128:, :], weight)
    for t in range(6):
        a, b = first[:, t * 128 : (t + 1) * 128], second[:, t * 128 : (t + 1) * 128]
        pair = (
            jnp.where(low, a, pltpu.roll(b, E, 1)),
            jnp.where(low, pltpu.roll(a, E, 1), b),
        )
        for k in range(2):
            g, h = (2 * t + k) // 3, (2 * t + k) % 3
            out[g, h] = pair[k].astype(BF)


def key_kernel(place_ref, x_ref, gain_ref, w_ref, normed_ref, *refs):
    normed_ref[...] = normalize(x_ref[...].astype(F32), gain_ref[...][None, :])
    outs, pieces = refs[:4], refs[4]
    write_pairs(normed_ref[...], w_ref[...], pieces)
    for s, out in enumerate(outs):
        out[:, 0] = pieces[(place_ref[X] + s) % 4]


def key_proj(place, x, gain, weight):
    piece = (3, 2, 128, 128)
    return pl.pallas_call(
        key_kernel,
        grid=(2,),
        in_specs=[
            SCALARS,
            pl.BlockSpec((256, 768), lambda i: (i, 0)),
            pl.BlockSpec((768,), lambda i: (0,)),
            pl.BlockSpec((768, 768), lambda i: (0, 1)),
        ],
        out_specs=[pl.BlockSpec((256, 768), lambda i: (i, 0))]
        + [pl.BlockSpec((3, 1, 128, 128), lambda i: (0, i, 0, 0))] * 4,
        out_shape=[jax.ShapeDtypeStruct((512, 768), BF)] + [jax.ShapeDtypeStruct(piece, BF)] * 4,
        scratch_shapes=[pltpu.VMEM((4, 3, 128, 128), BF)],
        compiler_params=params(52),
        name="key_proj",
    )(place, x, gain, weight)


def query_value_kernel(normed_ref, w_ref, out_ref):
    for rp in range(2):
        write_pairs(normed_ref[rp * 256 : (rp + 1) * 256, :], w_ref[...], out_ref.at[:, 0, :, rp])


def query_value_proj(normed, weight):
    return pl.pallas_call(
        query_value_kernel,
        grid=(2,),
        in_specs=[
            pl.BlockSpec((512, 768), lambda i: (0, 0)),
            pl.BlockSpec((768, 768), lambda i: (0, 2 * i)),
        ],
        out_specs=pl.BlockSpec((4, 1, 3, 2, 128, 128), lambda i: (0, i, 0, 0, 0, 0)),
        out_shape=jax.ShapeDtypeStruct((4, 2, 3, 2, 128, 128), BF),
        compiler_params=params(16),
        name="query_value_proj",
    )(normed, weight)


def over_x(pieces):
    return [pieces[0], send(pieces[3], dx=3), send(pieces[2], dx=2), send(pieces[1], dx=1)]


def scores_kernel(place_ref, q0_ref, q1_ref, *refs):
    own, keys_hbm, out_ref, keys, sems = refs[:8], *refs[8:]
    copies = [
        pltpu.make_async_copy(keys_hbm.at[z * 2 : z * 2 + 2], keys.at[z * 2 : z * 2 + 2, 1:], sems.at[z])
        for z in range(4)
    ]
    for copy in copies:
        copy.start()
    for i, block in enumerate(own):
        z = (place_ref[Z] + (0, 3, 1, 2)[i % 4]) % 4
        keys[z * 2 + (place_ref[CORE] + i // 4) % 2, 0] = block[...]
    left = [
        jnp.concatenate(
            [
                jnp.concatenate(
                    [
                        q[xh * 2 + xl, h, rp]
                        for q in (q0_ref, q1_ref)
                        for xl in range(2)
                        for rp in range(2)
                    ],
                    axis=1,
                )
                for xh in range(2)
            ],
            axis=0,
        )
        for h in range(3)
    ]
    for z in range(4):
        copies[z].wait()
        for h in range(3):
            right = [
                jnp.concatenate(
                    [
                        keys[z * 2 + (place_ref[CORE] + k) % 2, (xh * 2 + xl + 4 - place_ref[X]) % 4, h, rp]
                        for k in range(2)
                        for xl in range(2)
                        for rp in range(2)
                    ],
                    axis=1,
                )
                for xh in range(2)
            ]
            scores = mm_t(left[h], jnp.concatenate(right, axis=0))
            out_ref[:, h, :, z * 256 : (z + 1) * 256] = scores.reshape(4, 32, 256)


def partial_scores(place, q0, q1, own, keys):
    vmem = pl.BlockSpec(memory_space=pltpu.VMEM)
    return pl.pallas_call(
        scores_kernel,
        in_specs=[SCALARS] + [vmem] * 10 + [pl.BlockSpec(memory_space=pltpu.HBM)],
        out_specs=vmem,
        out_shape=jax.ShapeDtypeStruct((4, 3, 32, 1024), F32),
        scratch_shapes=[pltpu.VMEM((8, 4, 3, 2, 128, 128), BF), pltpu.SemaphoreType.DMA((4,))],
        compiler_params=params(48),
        name="partial_scores",
    )(place, q0, q1, *own, keys)


def softmax_kernel(scale, parts_ref, out_ref):
    tied = (parts_ref[0] + parts_ref[1] + parts_ref[2] + parts_ref[3]) * scale
    expo = jnp.exp(tied - jnp.max(tied, axis=-1, keepdims=True))
    out_ref[...] = (expo / jnp.sum(expo, axis=-1, keepdims=True)).astype(BF)


def row_softmax(parts, scale):
    return pl.pallas_call(
        lambda *refs: softmax_kernel(scale, *refs),
        in_specs=[pl.BlockSpec(memory_space=pltpu.VMEM)],
        out_specs=pl.BlockSpec(memory_space=pltpu.VMEM),
        out_shape=jax.ShapeDtypeStruct((3, 32, 1024), BF),
        compiler_params=params(8),
        name="row_softmax",
    )(parts)


def mix_kernel(place_ref, w0_ref, w1_ref, w2_ref, w3_ref, values_hbm, out_ref, weights, values, sems):
    order = [(c, xl) for c in range(2) for xl in range(2)]
    copies = [
        pltpu.make_async_copy(values_hbm.at[z * 2 + c, xh * 2 + xl], values.at[z * 2 + c, xh * 2 + xl], sems.at[i, z, xh])
        for i, (c, xl) in enumerate(order)
        for z in range(4)
        for xh in range(2)
    ]
    for copy in copies:
        copy.start()
    for d, w in enumerate((w0_ref, w1_ref, w2_ref, w3_ref)):
        share = (place_ref[Y] + d) % 4
        weights[:, pl.ds(pl.multiple_of(share * 32, 32), 32), :] = w[...]
    for i, (c, xl) in enumerate(order):
        for copy in copies[i * 8 : i * 8 + 8]:
            copy.wait()
        for h in range(3):
            right = [
                jnp.concatenate([values[z * 2 + c, xh * 2 + xl, h, rp] for rp in range(2)], axis=1)
                for z in range(4)
                for xh in range(2)
            ]
            mixed = mm(weights[h], jnp.concatenate(right, axis=0))
            pair = jnp.concatenate(
                [mixed[:, :128].reshape(16, 8, 128), mixed[:, 128:].reshape(16, 8, 128)], axis=1
            )
            out_ref[:, h, c, xl * 16 : (xl + 1) * 16, :] = pair.astype(BF)


def row_mix(place, weights, values):
    vmem = pl.BlockSpec(memory_space=pltpu.VMEM)
    return pl.pallas_call(
        mix_kernel,
        in_specs=[SCALARS] + [vmem] * 4 + [pl.BlockSpec(memory_space=pltpu.HBM)],
        out_specs=vmem,
        out_shape=jax.ShapeDtypeStruct((16, 3, 2, 32, 128), BF),
        scratch_shapes=[
            pltpu.VMEM((3, 128, 1024), BF),
            pltpu.VMEM(values.shape, BF),
            pltpu.SemaphoreType.DMA((4, 4, 2)),
        ],
        compiler_params=params(52),
        name="row_mix",
    )(place, *weights, values)


def column_kernel(
    mix_ref, x_ref, gain_col_ref, gain_ffn_ref, exit_row, exit_col, attend_hbm, expand_hbm, shrink_hbm,
    out_ref, qkv, stream, scratch, attend, expand, shrink, sems,
):
    copies = [
        pltpu.make_async_copy(attend_hbm, attend, sems.at[0]),
        pltpu.make_async_copy(expand_hbm, expand, sems.at[1]),
        pltpu.make_async_copy(shrink_hbm, shrink, sems.at[2]),
    ]
    for copy in copies:
        copy.start()
    low = lax.broadcasted_iota(jnp.int32, (64, 128), 1) < E
    halves = ([], [])
    for y in range(4):
        tiles = ([], [])
        for t in range(6):
            (g0, h0), (g1, h1) = divmod(2 * t, 3), divmod(2 * t + 1, 3)
            a = mix_ref[g0 * 4 + y, h0].astype(F32)
            b = mix_ref[g1 * 4 + y, h1].astype(F32)
            tiles[0].append(jnp.where(low, a, pltpu.roll(b, E, 1)).astype(BF))
            tiles[1].append(jnp.where(low, pltpu.roll(a, E, 1), b).astype(BF))
        for k in range(2):
            halves[k].append(jnp.concatenate(tiles[k], axis=1))
    exits = [mm(jnp.concatenate(halves[k], axis=0), exit_row[...]).reshape(32, 1, 8, 768) for k in range(2)]
    exits = jnp.concatenate(exits, axis=1).reshape(512, 768)
    x = jnp.concatenate([x_ref[(xl * 4 + y) * 2 + c] for y in range(4) for c in range(2) for xl in range(2)], axis=0)
    stream[...] = x.astype(F32) + exits

    normed = centre(stream[...]) * gain_col_ref[...][None, :]
    for t in range(6):
        scratch[t] = normed[:, t * 128 : (t + 1) * 128]
    normed = jnp.concatenate(
        [
            jnp.concatenate([scratch[t, pl.ds(c, 64, stride=8), :] for c in range(8)], axis=0).astype(BF)
            for t in range(6)
        ],
        axis=1,
    )
    copies[0].wait()
    qkv[...] = mm(normed, attend[...]).astype(BF)
    group = lax.broadcasted_iota(jnp.int32, (256, 256), 0) // E == lax.broadcasted_iota(jnp.int32, (256, 256), 1) // E
    group = group.astype(F32).astype(BF)
    zeros = jnp.zeros((E, 256), BF)

    def tile(part, c, g):
        return qkv[c * 64 : (c + 1) * 64, part * 768 + g * 256 : part * 768 + (g + 1) * 256]

    def by_head(part, c, g):
        return jnp.concatenate([tile(part, c, g)] * 4, axis=0) * group

    for c in range(0, 8, 2):
        for g in range(3):
            k = jnp.concatenate([by_head(1, c, g), by_head(1, c + 1, g)], axis=1)
            q = jnp.concatenate(
                [
                    jnp.concatenate([tile(0, c, g), zeros], axis=1),
                    jnp.concatenate([zeros, tile(0, c + 1, g)], axis=1),
                ],
                axis=0,
            )
            scores = (mm_t(k, q) * (E ** -0.5)).reshape(4, 64, 128)
            expo = jnp.exp(scores - jnp.max(scores, axis=1, keepdims=True))
            weights = expo * (1.0 / jnp.sum(expo, axis=1, keepdims=True))
            weights = weights.reshape(256, 128).astype(BF)
            for k in range(2):
                mixed = lax.dot_general(
                    weights, by_head(2, c + k, g), (((0,), (0,)), ((), ())), preferred_element_type=F32
                )
                for t in range(2):
                    scratch[g * 2 + t, pl.ds(c + k, 64, stride=8), :] = mixed[
                        k * 64 : (k + 1) * 64, t * 128 : (t + 1) * 128
                    ]
    mixed = jnp.concatenate([scratch[t].astype(BF) for t in range(6)], axis=1)
    stream[...] += mm(mixed, exit_col[...])

    normed = normalize(stream[...], gain_ffn_ref[...][None, :])
    copies[1].wait()
    copies[2].wait()
    for f in range(6):
        cols = slice(f * 512, (f + 1) * 512)
        pre = mm(normed, expand[:, cols])
        hidden = (0.5 * pre * (1.0 + lax.erf(pre * math.sqrt(0.5)))).astype(BF)
        stream[...] += mm(hidden, shrink[cols, :])
    done = stream[...].astype(BF)
    for i, (y, c, xl) in enumerate((y, c, xl) for y in range(4) for c in range(2) for xl in range(2)):
        out_ref[(xl * 4 + y) * 2 + c] = done[i * 32 : (i + 1) * 32, :]


def column_part(mix, x, gain_col, gain_ffn, exit_row, attend, exit_col, expand, shrink):
    vmem = pl.BlockSpec(memory_space=pltpu.VMEM)
    return pl.pallas_call(
        column_kernel,
        in_specs=[vmem] * 6 + [pl.BlockSpec(memory_space=pltpu.HBM)] * 3,
        out_specs=vmem,
        out_shape=jax.ShapeDtypeStruct((16, 32, 768), BF),
        scratch_shapes=[
            pltpu.VMEM((512, 2304), BF),
            pltpu.VMEM((512, 768), F32),
            pltpu.VMEM((6, 512, 128), F32),
            pltpu.VMEM(attend.shape, BF),
            pltpu.VMEM(expand.shape, BF),
            pltpu.VMEM(shrink.shape, BF),
            pltpu.SemaphoreType.DMA((3,)),
        ],
        compiler_params=params(48),
        name="column_part",
    )(mix, x, gain_col, gain_ffn, exit_row, exit_col, attend, expand, shrink)


def local(
    embeddings,
    gain_row,
    attend_row,
    exit_row,
    gain_col,
    attend_col,
    exit_col,
    gain_ffn,
    expand,
    shrink,
):
    seq, col = lax.axis_index("seq"), lax.axis_index("col")
    core, y, z = seq % 2, seq // 2 % 4, col // 2
    place = jnp.stack([core, col % 2 * 2 + seq // 8, y, z]).astype(jnp.int32)
    scale = E ** (-0.5) / math.sqrt(embeddings.shape[0] * lax.axis_size("seq"))

    normed, *keys = key_proj(place, embeddings.reshape(512, 768), gain_row, attend_row)
    keys = over_x(keys)
    queries_values = query_value_proj(normed, attend_row)
    x = embeddings.reshape(4, 2, 8, 8, 768).transpose(2, 1, 0, 3, 4).reshape(16, 32, 768)
    own, *keys = keys
    keys, own, queries_values = lax.optimization_barrier((jnp.stack(keys), own, queries_values))

    keys_all = gather(keys, Z_COLUMNS)
    own = [own] + [send(own, dz=dz) for dz in (1, 3, 2)]
    queries_values, x = lax.optimization_barrier((swap(queries_values, X_RINGS), x, *own))[:2]
    own = own + [to_other_core(k) for k in own]
    x = lax.all_to_all(x, "seq", split_axis=0, concat_axis=0, tiled=True)
    queries, values = queries_values[:, 0], queries_values[:, 1]
    values = lax.optimization_barrier((values, keys))[0]
    values = gather(values, Z_COLUMNS)

    queries0 = lax.dynamic_slice_in_dim(queries, core * 64, 64, axis=3)
    queries1 = to_other_core(lax.dynamic_slice_in_dim(queries, (1 - core) * 64, 64, axis=3))
    keys = lax.optimization_barrier((keys_all, x, queries1, *own))[0]
    scores = partial_scores(place, queries0, queries1, own, keys)
    scores, x = lax.optimization_barrier((scores, x))
    weights = row_softmax(swap(scores, Y_RINGS), scale)
    values = lax.optimization_barrier((values, weights))[0]
    weights = [weights] + [send(weights, dy=dy) for dy in (3, 2, 1)]
    mix = row_mix(place, weights, values)
    mix = swap(mix, PLANES).reshape(16, 3, 64, 128)

    out = column_part(mix, x, gain_col, gain_ffn, exit_row, attend_col, exit_col, expand, shrink)
    out = lax.all_to_all(out, "seq", split_axis=0, concat_axis=0, tiled=True)
    return out.reshape(8, 2, 4, 8, 768).transpose(2, 1, 0, 3, 4).reshape(4, 128, 768)


def solution(mesh):
    in_specs = (P("seq", "col", None), P(), P(), P(), P(), P(), P(), P(), P(), P())
    out_specs = P("seq", "col", None)
    return jax.shard_map(local, mesh=mesh, in_specs=in_specs, out_specs=out_specs, check_vma=False)
```

```python
import math

import jax
import jax.numpy as jnp
from jax import lax
from jax.experimental import pallas as pl
from jax.experimental.pallas import tpu as pltpu
from jax.sharding import PartitionSpec as P

AXES = ("seq", "col")
HEADS = 12
E = 64
BF = jnp.bfloat16
F32 = jnp.float32


def device(xl, y, c, z, xh):
    return ((xl * 4 + y) * 2 + c) * 8 + z * 2 + xh


R2, R4 = range(2), range(4)
Y_RINGS = [[device(xl, y, c, z, xh) for y in R4] for xl in R2 for c in R2 for z in R4 for xh in R2]
Z_COLUMNS = [[device(xl, y, c, z, xh) for z in R4 for c in R2] for xl in R2 for y in R4 for xh in R2]
X_RINGS = [[device(xl, y, c, z, xh) for xh in R2 for xl in R2] for y in R4 for c in R2 for z in R4]
PLANES = [[device(xl, y, c, z, xh) for xh in R2 for xl in R2 for y in R4] for c in R2 for z in R4]


def shifts(dx=0, dy=0, dz=0, dc=0):
    pairs = []
    for x in R4:
        for y in R4:
            for c in R2:
                for z in R4:
                    to = ((x + dx) % 4, (y + dy) % 4, (c + dc) % 2, (z + dz) % 4)
                    pairs.append((device(x % 2, y, c, z, x // 2), device(to[0] % 2, *to[1:], to[0] // 2)))
    return pairs


def params(mib):
    return pltpu.CompilerParams(vmem_limit_bytes=mib * 1024 * 1024)


def swap(array, groups):
    return lax.all_to_all(array, AXES, split_axis=0, concat_axis=0, tiled=True, axis_index_groups=groups)


def gather(array, groups):
    return lax.all_gather(array, AXES, axis=0, tiled=False, axis_index_groups=groups)


def send(array, **by):
    return lax.ppermute(array, AXES, shifts(**by))


def to_other_core(array):
    return send(array, dc=1)


def mm(a, b):
    return jnp.dot(a, b, preferred_element_type=F32)


def mm_t(a, b):
    return lax.dot_general(a, b, (((1,), (1,)), ((), ())), preferred_element_type=F32)


def centre(stream):
    mean = jnp.mean(stream, axis=-1, keepdims=True)
    centred = stream - mean
    var = jnp.mean(centred * centred, axis=-1, keepdims=True)
    return centred * lax.rsqrt(var + 1e-05)


def normalize(stream, gain):
    return (centre(stream) * gain).astype(BF)


CORE, X, Y, Z = range(4)
SCALARS = pl.BlockSpec(memory_space=pltpu.SMEM)


def write_pairs(normed, weight, out):
    low = lax.broadcasted_iota(jnp.int32, (128, 128), 1) < E
    first, second = mm(normed[:128, :], weight), mm(normed[128:, :], weight)
    for t in range(6):
        a, b = first[:, t * 128 : (t + 1) * 128], second[:, t * 128 : (t + 1) * 128]
        pair = (
            jnp.where(low, a, pltpu.roll(b, E, 1)),
            jnp.where(low, pltpu.roll(a, E, 1), b),
        )
        for k in range(2):
            g, h = (2 * t + k) // 3, (2 * t + k) % 3
            out[g, h] = pair[k].astype(BF)


def key_kernel(place_ref, x_ref, gain_ref, w_ref, normed_ref, *refs):
    normed_ref[...] = normalize(x_ref[...].astype(F32), gain_ref[...][None, :])
    outs, pieces = refs[:4], refs[4]
    write_pairs(normed_ref[...], w_ref[...], pieces)
    for s, out in enumerate(outs):
        out[:, 0] = pieces[(place_ref[X] + s) % 4]


def key_proj(place, x, gain, weight):
    piece = (3, 2, 128, 128)
    return pl.pallas_call(
        key_kernel,
        grid=(2,),
        in_specs=[
            SCALARS,
            pl.BlockSpec((256, 768), lambda i: (i, 0)),
            pl.BlockSpec((768,), lambda i: (0,)),
            pl.BlockSpec((768, 768), lambda i: (0, 1)),
        ],
        out_specs=[pl.BlockSpec((256, 768), lambda i: (i, 0))]
        + [pl.BlockSpec((3, 1, 128, 128), lambda i: (0, i, 0, 0))] * 4,
        out_shape=[jax.ShapeDtypeStruct((512, 768), BF)] + [jax.ShapeDtypeStruct(piece, BF)] * 4,
        scratch_shapes=[pltpu.VMEM((4, 3, 128, 128), BF)],
        compiler_params=params(52),
        name="key_proj",
    )(place, x, gain, weight)


def query_value_kernel(normed_ref, w_ref, out_ref):
    for rp in range(2):
        write_pairs(normed_ref[rp * 256 : (rp + 1) * 256, :], w_ref[...], out_ref.at[:, 0, :, rp])


def query_value_proj(normed, weight):
    return pl.pallas_call(
        query_value_kernel,
        grid=(2,),
        in_specs=[
            pl.BlockSpec((512, 768), lambda i: (0, 0)),
            pl.BlockSpec((768, 768), lambda i: (0, 2 * i)),
        ],
        out_specs=pl.BlockSpec((4, 1, 3, 2, 128, 128), lambda i: (0, i, 0, 0, 0, 0)),
        out_shape=jax.ShapeDtypeStruct((4, 2, 3, 2, 128, 128), BF),
        compiler_params=params(16),
        name="query_value_proj",
    )(normed, weight)


def over_x(pieces):
    return [pieces[0], send(pieces[3], dx=3), send(pieces[2], dx=2), send(pieces[1], dx=1)]


def scores_kernel(place_ref, q0_ref, q1_ref, *refs):
    own, keys_hbm, out_ref, keys, sems = refs[:8], *refs[8:]
    copies = [
        pltpu.make_async_copy(keys_hbm.at[z * 2 : z * 2 + 2], keys.at[z * 2 : z * 2 + 2, 1:], sems.at[z])
        for z in range(4)
    ]
    for copy in copies:
        copy.start()
    for i, block in enumerate(own):
        z = (place_ref[Z] + (0, 3, 1, 2)[i % 4]) % 4
        keys[z * 2 + (place_ref[CORE] + i // 4) % 2, 0] = block[...]
    left = [
        jnp.concatenate(
            [
                jnp.concatenate(
                    [
                        q[xh * 2 + xl, h, rp]
                        for q in (q0_ref, q1_ref)
                        for xl in range(2)
                        for rp in range(2)
                    ],
                    axis=1,
                )
                for xh in range(2)
            ],
            axis=0,
        )
        for h in range(3)
    ]
    for z in range(4):
        copies[z].wait()
        for h in range(3):
            right = [
                jnp.concatenate(
                    [
                        keys[z * 2 + (place_ref[CORE] + k) % 2, (xh * 2 + xl + 4 - place_ref[X]) % 4, h, rp]
                        for k in range(2)
                        for xl in range(2)
                        for rp in range(2)
                    ],
                    axis=1,
                )
                for xh in range(2)
            ]
            scores = mm_t(left[h], jnp.concatenate(right, axis=0))
            out_ref[:, h, :, z * 256 : (z + 1) * 256] = scores.reshape(4, 32, 256)


def partial_scores(place, q0, q1, own, keys):
    vmem = pl.BlockSpec(memory_space=pltpu.VMEM)
    return pl.pallas_call(
        scores_kernel,
        in_specs=[SCALARS] + [vmem] * 10 + [pl.BlockSpec(memory_space=pltpu.HBM)],
        out_specs=vmem,
        out_shape=jax.ShapeDtypeStruct((4, 3, 32, 1024), F32),
        scratch_shapes=[pltpu.VMEM((8, 4, 3, 2, 128, 128), BF), pltpu.SemaphoreType.DMA((4,))],
        compiler_params=params(48),
        name="partial_scores",
    )(place, q0, q1, *own, keys)


def softmax_kernel(scale, parts_ref, out_ref):
    tied = (parts_ref[0] + parts_ref[1] + parts_ref[2] + parts_ref[3]) * scale
    expo = jnp.exp(tied - jnp.max(tied, axis=-1, keepdims=True))
    out_ref[...] = (expo / jnp.sum(expo, axis=-1, keepdims=True)).astype(BF)


def row_softmax(parts, scale):
    return pl.pallas_call(
        lambda *refs: softmax_kernel(scale, *refs),
        in_specs=[pl.BlockSpec(memory_space=pltpu.VMEM)],
        out_specs=pl.BlockSpec(memory_space=pltpu.VMEM),
        out_shape=jax.ShapeDtypeStruct((3, 32, 1024), BF),
        compiler_params=params(8),
        name="row_softmax",
    )(parts)


def mix_kernel(place_ref, w0_ref, w1_ref, w2_ref, w3_ref, values_hbm, out_ref, weights, values, sems):
    order = [(c, xl) for c in range(2) for xl in range(2)]
    copies = [
        pltpu.make_async_copy(values_hbm.at[z * 2 + c, xh * 2 + xl], values.at[z * 2 + c, xh * 2 + xl], sems.at[i, z, xh])
        for i, (c, xl) in enumerate(order)
        for z in range(4)
        for xh in range(2)
    ]
    for copy in copies:
        copy.start()
    for d, w in enumerate((w0_ref, w1_ref, w2_ref, w3_ref)):
        share = (place_ref[Y] + d) % 4
        weights[:, pl.ds(pl.multiple_of(share * 32, 32), 32), :] = w[...]
    for i, (c, xl) in enumerate(order):
        for copy in copies[i * 8 : i * 8 + 8]:
            copy.wait()
        for h in range(3):
            right = [
                jnp.concatenate([values[z * 2 + c, xh * 2 + xl, h, rp] for rp in range(2)], axis=1)
                for z in range(4)
                for xh in range(2)
            ]
            mixed = mm(weights[h], jnp.concatenate(right, axis=0))
            pair = jnp.concatenate(
                [mixed[:, :128].reshape(16, 8, 128), mixed[:, 128:].reshape(16, 8, 128)], axis=1
            )
            out_ref[:, h, c, xl * 16 : (xl + 1) * 16, :] = pair.astype(BF)


def row_mix(place, weights, values):
    vmem = pl.BlockSpec(memory_space=pltpu.VMEM)
    return pl.pallas_call(
        mix_kernel,
        in_specs=[SCALARS] + [vmem] * 4 + [pl.BlockSpec(memory_space=pltpu.HBM)],
        out_specs=vmem,
        out_shape=jax.ShapeDtypeStruct((16, 3, 2, 32, 128), BF),
        scratch_shapes=[
            pltpu.VMEM((3, 128, 1024), BF),
            pltpu.VMEM(values.shape, BF),
            pltpu.SemaphoreType.DMA((4, 4, 2)),
        ],
        compiler_params=params(52),
        name="row_mix",
    )(place, *weights, values)


def column_kernel(
    mix_ref, x_ref, gain_col_ref, gain_ffn_ref, exit_row, exit_col, attend, expand_hbm, shrink_hbm,
    out_ref, qkv, stream, scratch, expand, shrink, sems,
):
    copies = [
        pltpu.make_async_copy(expand_hbm, expand, sems.at[0]),
        pltpu.make_async_copy(shrink_hbm, shrink, sems.at[1]),
    ]
    for copy in copies:
        copy.start()
    low = lax.broadcasted_iota(jnp.int32, (64, 128), 1) < E
    halves = ([], [])
    for y in range(4):
        tiles = ([], [])
        for t in range(6):
            (g0, h0), (g1, h1) = divmod(2 * t, 3), divmod(2 * t + 1, 3)
            a = mix_ref[g0 * 4 + y, h0].astype(F32)
            b = mix_ref[g1 * 4 + y, h1].astype(F32)
            tiles[0].append(jnp.where(low, a, pltpu.roll(b, E, 1)).astype(BF))
            tiles[1].append(jnp.where(low, pltpu.roll(a, E, 1), b).astype(BF))
        for k in range(2):
            halves[k].append(jnp.concatenate(tiles[k], axis=1))
    exits = [mm(jnp.concatenate(halves[k], axis=0), exit_row[...]).reshape(32, 1, 8, 768) for k in range(2)]
    exits = jnp.concatenate(exits, axis=1).reshape(512, 768)
    x = jnp.concatenate([x_ref[(xl * 4 + y) * 2 + c] for y in range(4) for c in range(2) for xl in range(2)], axis=0)
    stream[...] = x.astype(F32) + exits

    normed = centre(stream[...]) * gain_col_ref[...][None, :]
    for t in range(6):
        scratch[t] = normed[:, t * 128 : (t + 1) * 128]
    normed = jnp.concatenate(
        [
            jnp.concatenate([scratch[t, pl.ds(c, 64, stride=8), :] for c in range(8)], axis=0).astype(BF)
            for t in range(6)
        ],
        axis=1,
    )
    qkv[...] = mm(normed, attend[...]).astype(BF)
    group = lax.broadcasted_iota(jnp.int32, (256, 256), 0) // E == lax.broadcasted_iota(jnp.int32, (256, 256), 1) // E
    group = group.astype(F32).astype(BF)
    zeros = jnp.zeros((E, 256), BF)

    def tile(part, c, g):
        return qkv[c * 64 : (c + 1) * 64, part * 768 + g * 256 : part * 768 + (g + 1) * 256]

    def by_head(part, c, g):
        return jnp.concatenate([tile(part, c, g)] * 4, axis=0) * group

    for c in range(0, 8, 2):
        for g in range(3):
            k = jnp.concatenate([by_head(1, c, g), by_head(1, c + 1, g)], axis=1)
            q = jnp.concatenate(
                [
                    jnp.concatenate([tile(0, c, g), zeros], axis=1),
                    jnp.concatenate([zeros, tile(0, c + 1, g)], axis=1),
                ],
                axis=0,
            )
            scores = (mm_t(k, q) * (E ** -0.5)).reshape(4, 64, 128)
            expo = jnp.exp(scores - jnp.max(scores, axis=1, keepdims=True))
            weights = expo * (1.0 / jnp.sum(expo, axis=1, keepdims=True))
            weights = weights.reshape(256, 128).astype(BF)
            for k in range(2):
                mixed = lax.dot_general(
                    weights, by_head(2, c + k, g), (((0,), (0,)), ((), ())), preferred_element_type=F32
                )
                for t in range(2):
                    scratch[g * 2 + t, pl.ds(c + k, 64, stride=8), :] = mixed[
                        k * 64 : (k + 1) * 64, t * 128 : (t + 1) * 128
                    ]
    mixed = jnp.concatenate([scratch[t].astype(BF) for t in range(6)], axis=1)
    stream[...] += mm(mixed, exit_col[...])

    normed = normalize(stream[...], gain_ffn_ref[...][None, :])
    for copy in copies:
        copy.wait()
    for r in range(4):
        rows = slice(r * 128, (r + 1) * 128)
        pre = mm(normed[rows, :], expand[...])
        hidden = (0.5 * pre * (1.0 + lax.erf(pre * math.sqrt(0.5)))).astype(BF)
        stream[rows, :] += mm(hidden, shrink[...])
    done = stream[...].astype(BF)
    for i, (y, c, xl) in enumerate((y, c, xl) for y in range(4) for c in range(2) for xl in range(2)):
        out_ref[(xl * 4 + y) * 2 + c] = done[i * 32 : (i + 1) * 32, :]


def column_part(mix, x, gain_col, gain_ffn, exit_row, attend, exit_col, expand, shrink):
    vmem = pl.BlockSpec(memory_space=pltpu.VMEM)
    return pl.pallas_call(
        column_kernel,
        in_specs=[vmem] * 7 + [pl.BlockSpec(memory_space=pltpu.HBM)] * 2,
        out_specs=vmem,
        out_shape=jax.ShapeDtypeStruct((16, 32, 768), BF),
        scratch_shapes=[
            pltpu.VMEM((512, 2304), BF),
            pltpu.VMEM((512, 768), F32),
            pltpu.VMEM((6, 512, 128), F32),
            pltpu.VMEM(expand.shape, BF),
            pltpu.VMEM(shrink.shape, BF),
            pltpu.SemaphoreType.DMA((2,)),
        ],
        compiler_params=params(44),
        name="column_part",
    )(mix, x, gain_col, gain_ffn, exit_row, exit_col, attend, expand, shrink)


def local(
    embeddings,
    gain_row,
    attend_row,
    exit_row,
    gain_col,
    attend_col,
    exit_col,
    gain_ffn,
    expand,
    shrink,
):
    seq, col = lax.axis_index("seq"), lax.axis_index("col")
    core, y, z = seq % 2, seq // 2 % 4, col // 2
    place = jnp.stack([core, col % 2 * 2 + seq // 8, y, z]).astype(jnp.int32)
    scale = E ** (-0.5) / math.sqrt(embeddings.shape[0] * lax.axis_size("seq"))

    normed, *keys = key_proj(place, embeddings.reshape(512, 768), gain_row, attend_row)
    keys = over_x(keys)
    queries_values = query_value_proj(normed, attend_row)
    x = embeddings.reshape(4, 2, 8, 8, 768).transpose(2, 1, 0, 3, 4).reshape(16, 32, 768)
    own, *keys = keys
    keys, own, queries_values = lax.optimization_barrier((jnp.stack(keys), own, queries_values))

    keys_all = gather(keys, Z_COLUMNS)
    own = [own] + [send(own, dz=dz) for dz in (1, 3, 2)]
    queries_values, x = lax.optimization_barrier((swap(queries_values, X_RINGS), x, *own))[:2]
    own = own + [to_other_core(k) for k in own]
    x = lax.all_to_all(x, "seq", split_axis=0, concat_axis=0, tiled=True)
    queries, values = queries_values[:, 0], queries_values[:, 1]
    values = lax.optimization_barrier((values, keys))[0]
    values = gather(values, Z_COLUMNS)

    queries0 = lax.dynamic_slice_in_dim(queries, core * 64, 64, axis=3)
    queries1 = to_other_core(lax.dynamic_slice_in_dim(queries, (1 - core) * 64, 64, axis=3))
    keys = lax.optimization_barrier((keys_all, x, queries1, *own))[0]
    scores = partial_scores(place, queries0, queries1, own, keys)
    scores, x = lax.optimization_barrier((scores, x))
    weights = row_softmax(swap(scores, Y_RINGS), scale)
    values = lax.optimization_barrier((values, weights))[0]
    weights = [weights] + [send(weights, dy=dy) for dy in (3, 2, 1)]
    mix = row_mix(place, weights, values)
    mix = swap(mix, PLANES).reshape(16, 3, 64, 128)

    out = column_part(mix, x, gain_col, gain_ffn, exit_row, attend_col, exit_col, expand, shrink)
    out = lax.all_to_all(out, "seq", split_axis=0, concat_axis=0, tiled=True)
    return out.reshape(8, 2, 4, 8, 768).transpose(2, 1, 0, 3, 4).reshape(4, 128, 768)


def solution(mesh):
    in_specs = (P("seq", "col", None), P(), P(), P(), P(), P(), P(), P(), P(), P())
    out_specs = P("seq", "col", None)
    return jax.shard_map(local, mesh=mesh, in_specs=in_specs, out_specs=out_specs, check_vma=False)
```

```python
import math

import jax
import jax.numpy as jnp
from jax import lax
from jax.experimental import pallas as pl
from jax.experimental.pallas import tpu as pltpu
from jax.sharding import PartitionSpec as P

AXES = ("seq", "col")
HEADS = 12
E = 64
BF = jnp.bfloat16
F32 = jnp.float32


def device(xl, y, c, z, xh):
    return ((xl * 4 + y) * 2 + c) * 8 + z * 2 + xh


R2, R4 = range(2), range(4)
Y_RINGS = [[device(xl, y, c, z, xh) for y in R4] for xl in R2 for c in R2 for z in R4 for xh in R2]
Z_COLUMNS = [[device(xl, y, c, z, xh) for z in R4 for c in R2] for xl in R2 for y in R4 for xh in R2]
X_RINGS = [[device(xl, y, c, z, xh) for xh in R2 for xl in R2] for y in R4 for c in R2 for z in R4]
PLANES = [[device(xl, y, c, z, xh) for xh in R2 for xl in R2 for y in R4] for c in R2 for z in R4]


def shifts(dx=0, dy=0, dz=0, dc=0):
    pairs = []
    for x in R4:
        for y in R4:
            for c in R2:
                for z in R4:
                    to = ((x + dx) % 4, (y + dy) % 4, (c + dc) % 2, (z + dz) % 4)
                    pairs.append((device(x % 2, y, c, z, x // 2), device(to[0] % 2, *to[1:], to[0] // 2)))
    return pairs


def params(mib):
    return pltpu.CompilerParams(vmem_limit_bytes=mib * 1024 * 1024)


def swap(array, groups):
    return lax.all_to_all(array, AXES, split_axis=0, concat_axis=0, tiled=True, axis_index_groups=groups)


def gather(array, groups):
    return lax.all_gather(array, AXES, axis=0, tiled=False, axis_index_groups=groups)


def send(array, **by):
    return lax.ppermute(array, AXES, shifts(**by))


def to_other_core(array):
    return send(array, dc=1)


def mm(a, b):
    return jnp.dot(a, b, preferred_element_type=F32)


def mm_t(a, b):
    return lax.dot_general(a, b, (((1,), (1,)), ((), ())), preferred_element_type=F32)


def centre(stream):
    mean = jnp.mean(stream, axis=-1, keepdims=True)
    centred = stream - mean
    var = jnp.mean(centred * centred, axis=-1, keepdims=True)
    return centred * lax.rsqrt(var + 1e-05)


def normalize(stream, gain):
    return (centre(stream) * gain).astype(BF)


CORE, X, Y, Z = range(4)
SCALARS = pl.BlockSpec(memory_space=pltpu.SMEM)


def write_pairs(normed, weight, out):
    low = lax.broadcasted_iota(jnp.int32, (128, 128), 1) < E
    first, second = mm(normed[:128, :], weight), mm(normed[128:, :], weight)
    for t in range(6):
        a, b = first[:, t * 128 : (t + 1) * 128], second[:, t * 128 : (t + 1) * 128]
        pair = (
            jnp.where(low, a, pltpu.roll(b, E, 1)),
            jnp.where(low, pltpu.roll(a, E, 1), b),
        )
        for k in range(2):
            g, h = (2 * t + k) // 3, (2 * t + k) % 3
            out[g, h] = pair[k].astype(BF)


def key_kernel(place_ref, x_ref, gain_ref, w_ref, normed_ref, *refs):
    normed_ref[...] = normalize(x_ref[...].astype(F32), gain_ref[...][None, :])
    outs, pieces = refs[:4], refs[4]
    write_pairs(normed_ref[...], w_ref[...], pieces)
    for s, out in enumerate(outs):
        out[:, 0] = pieces[(place_ref[X] + s) % 4]


def key_proj(place, x, gain, weight):
    piece = (3, 2, 128, 128)
    return pl.pallas_call(
        key_kernel,
        grid=(2,),
        in_specs=[
            SCALARS,
            pl.BlockSpec((256, 768), lambda i: (i, 0)),
            pl.BlockSpec((768,), lambda i: (0,)),
            pl.BlockSpec((768, 768), lambda i: (0, 1)),
        ],
        out_specs=[pl.BlockSpec((256, 768), lambda i: (i, 0))]
        + [pl.BlockSpec((3, 1, 128, 128), lambda i: (0, i, 0, 0))] * 4,
        out_shape=[jax.ShapeDtypeStruct((512, 768), BF)] + [jax.ShapeDtypeStruct(piece, BF)] * 4,
        scratch_shapes=[pltpu.VMEM((4, 3, 128, 128), BF)],
        compiler_params=params(52),
        name="key_proj",
    )(place, x, gain, weight)


def query_value_kernel(normed_ref, w_ref, out_ref):
    for rp in range(2):
        write_pairs(normed_ref[rp * 256 : (rp + 1) * 256, :], w_ref[...], out_ref.at[:, 0, :, rp])


def query_value_proj(normed, weight):
    return pl.pallas_call(
        query_value_kernel,
        grid=(2,),
        in_specs=[
            pl.BlockSpec((512, 768), lambda i: (0, 0)),
            pl.BlockSpec((768, 768), lambda i: (0, 2 * i)),
        ],
        out_specs=pl.BlockSpec((4, 1, 3, 2, 128, 128), lambda i: (0, i, 0, 0, 0, 0)),
        out_shape=jax.ShapeDtypeStruct((4, 2, 3, 2, 128, 128), BF),
        compiler_params=params(16),
        name="query_value_proj",
    )(normed, weight)


def over_x(pieces):
    return [pieces[0], send(pieces[3], dx=3), send(pieces[2], dx=2), send(pieces[1], dx=1)]


def scores_kernel(place_ref, q0_ref, q1_ref, *refs):
    own, keys_hbm, out_ref, keys, sems = refs[:8], *refs[8:]
    copies = [
        pltpu.make_async_copy(keys_hbm.at[z * 2 : z * 2 + 2], keys.at[z * 2 : z * 2 + 2, 1:], sems.at[z])
        for z in range(4)
    ]
    for copy in copies:
        copy.start()
    for i, block in enumerate(own):
        z = (place_ref[Z] + (0, 3, 1, 2)[i % 4]) % 4
        keys[z * 2 + (place_ref[CORE] + i // 4) % 2, 0] = block[...]
    left = [
        jnp.concatenate(
            [
                jnp.concatenate(
                    [
                        q[xh * 2 + xl, h, rp]
                        for q in (q0_ref, q1_ref)
                        for xl in range(2)
                        for rp in range(2)
                    ],
                    axis=1,
                )
                for xh in range(2)
            ],
            axis=0,
        )
        for h in range(3)
    ]
    for z in range(4):
        copies[z].wait()
        for h in range(3):
            right = [
                jnp.concatenate(
                    [
                        keys[z * 2 + (place_ref[CORE] + k) % 2, (xh * 2 + xl + 4 - place_ref[X]) % 4, h, rp]
                        for k in range(2)
                        for xl in range(2)
                        for rp in range(2)
                    ],
                    axis=1,
                )
                for xh in range(2)
            ]
            scores = mm_t(left[h], jnp.concatenate(right, axis=0))
            out_ref[:, h, :, z * 256 : (z + 1) * 256] = scores.reshape(4, 32, 256)


def partial_scores(place, q0, q1, own, keys):
    vmem = pl.BlockSpec(memory_space=pltpu.VMEM)
    return pl.pallas_call(
        scores_kernel,
        in_specs=[SCALARS] + [vmem] * 10 + [pl.BlockSpec(memory_space=pltpu.HBM)],
        out_specs=vmem,
        out_shape=jax.ShapeDtypeStruct((4, 3, 32, 1024), F32),
        scratch_shapes=[pltpu.VMEM((8, 4, 3, 2, 128, 128), BF), pltpu.SemaphoreType.DMA((4,))],
        compiler_params=params(48),
        name="partial_scores",
    )(place, q0, q1, *own, keys)


def softmax_kernel(scale, parts_ref, out_ref):
    tied = (parts_ref[0] + parts_ref[1] + parts_ref[2] + parts_ref[3]) * scale
    expo = jnp.exp(tied - jnp.max(tied, axis=-1, keepdims=True))
    out_ref[...] = (expo / jnp.sum(expo, axis=-1, keepdims=True)).astype(BF)


def row_softmax(parts, scale):
    return pl.pallas_call(
        lambda *refs: softmax_kernel(scale, *refs),
        in_specs=[pl.BlockSpec(memory_space=pltpu.VMEM)],
        out_specs=pl.BlockSpec(memory_space=pltpu.VMEM),
        out_shape=jax.ShapeDtypeStruct((3, 32, 1024), BF),
        compiler_params=params(8),
        name="row_softmax",
    )(parts)


def mix_kernel(place_ref, w0_ref, w1_ref, w2_ref, w3_ref, values_hbm, out_ref, weights, values, sems):
    order = [(c, xl) for c in range(2) for xl in range(2)]
    copies = [
        pltpu.make_async_copy(values_hbm.at[z * 2 + c, xh * 2 + xl], values.at[z * 2 + c, xh * 2 + xl], sems.at[i, z, xh])
        for i, (c, xl) in enumerate(order)
        for z in range(4)
        for xh in range(2)
    ]
    for copy in copies:
        copy.start()
    for d, w in enumerate((w0_ref, w1_ref, w2_ref, w3_ref)):
        share = (place_ref[Y] + d) % 4
        weights[:, pl.ds(pl.multiple_of(share * 32, 32), 32), :] = w[...]
    for i, (c, xl) in enumerate(order):
        for copy in copies[i * 8 : i * 8 + 8]:
            copy.wait()
        for h in range(3):
            right = [
                jnp.concatenate([values[z * 2 + c, xh * 2 + xl, h, rp] for rp in range(2)], axis=1)
                for z in range(4)
                for xh in range(2)
            ]
            mixed = mm(weights[h], jnp.concatenate(right, axis=0))
            pair = jnp.concatenate(
                [mixed[:, :128].reshape(16, 8, 128), mixed[:, 128:].reshape(16, 8, 128)], axis=1
            )
            out_ref[:, h, c, xl * 16 : (xl + 1) * 16, :] = pair.astype(BF)


def row_mix(place, weights, values):
    vmem = pl.BlockSpec(memory_space=pltpu.VMEM)
    return pl.pallas_call(
        mix_kernel,
        in_specs=[SCALARS] + [vmem] * 4 + [pl.BlockSpec(memory_space=pltpu.HBM)],
        out_specs=vmem,
        out_shape=jax.ShapeDtypeStruct((16, 3, 2, 32, 128), BF),
        scratch_shapes=[
            pltpu.VMEM((3, 128, 1024), BF),
            pltpu.VMEM(values.shape, BF),
            pltpu.SemaphoreType.DMA((4, 4, 2)),
        ],
        compiler_params=params(52),
        name="row_mix",
    )(place, *weights, values)


def column_kernel(
    mix_ref, x_ref, gain_col_ref, gain_ffn_ref, exit_row, exit_col, attend, expand_hbm, shrink_hbm,
    out_ref, qkv, stream, scratch, expand, shrink, sems,
):
    copies = [
        pltpu.make_async_copy(expand_hbm, expand, sems.at[0]),
        pltpu.make_async_copy(shrink_hbm, shrink, sems.at[1]),
    ]
    for copy in copies:
        copy.start()
    low = lax.broadcasted_iota(jnp.int32, (64, 128), 1) < E
    halves = ([], [])
    for y in range(4):
        tiles = ([], [])
        for t in range(6):
            (g0, h0), (g1, h1) = divmod(2 * t, 3), divmod(2 * t + 1, 3)
            a = mix_ref[g0 * 4 + y, h0].astype(F32)
            b = mix_ref[g1 * 4 + y, h1].astype(F32)
            tiles[0].append(jnp.where(low, a, pltpu.roll(b, E, 1)).astype(BF))
            tiles[1].append(jnp.where(low, pltpu.roll(a, E, 1), b).astype(BF))
        for k in range(2):
            halves[k].append(jnp.concatenate(tiles[k], axis=1))
    exits = [mm(jnp.concatenate(halves[k], axis=0), exit_row[...]).reshape(32, 1, 8, 768) for k in range(2)]
    exits = jnp.concatenate(exits, axis=1).reshape(512, 768)
    x = jnp.concatenate([x_ref[(xl * 4 + y) * 2 + c] for y in range(4) for c in range(2) for xl in range(2)], axis=0)
    stream[...] = x.astype(F32) + exits

    normed = centre(stream[...]) * gain_col_ref[...][None, :]
    for t in range(6):
        scratch[t] = normed[:, t * 128 : (t + 1) * 128]
    normed = jnp.concatenate(
        [
            jnp.concatenate([scratch[t, pl.ds(c, 64, stride=8), :] for c in range(8)], axis=0).astype(BF)
            for t in range(6)
        ],
        axis=1,
    )
    qkv[...] = mm(normed, attend[...]).astype(BF)
    group = lax.broadcasted_iota(jnp.int32, (256, 256), 0) // E == lax.broadcasted_iota(jnp.int32, (256, 256), 1) // E
    group = group.astype(F32).astype(BF)
    zeros = jnp.zeros((E, 256), BF)

    def tile(part, c, g):
        return qkv[c * 64 : (c + 1) * 64, part * 768 + g * 256 : part * 768 + (g + 1) * 256]

    def by_head(part, c, g):
        return jnp.concatenate([tile(part, c, g)] * 4, axis=0) * group

    for c in range(0, 8, 2):
        for g in range(3):
            k = jnp.concatenate([by_head(1, c, g), by_head(1, c + 1, g)], axis=1)
            q = jnp.concatenate(
                [
                    jnp.concatenate([tile(0, c, g), zeros], axis=1),
                    jnp.concatenate([zeros, tile(0, c + 1, g)], axis=1),
                ],
                axis=0,
            )
            scores = (mm_t(k, q) * (E ** -0.5)).reshape(4, 64, 128)
            expo = jnp.exp(scores - jnp.max(scores, axis=1, keepdims=True))
            weights = expo * (1.0 / jnp.sum(expo, axis=1, keepdims=True))
            weights = weights.reshape(256, 128).astype(BF)
            for k in range(2):
                mixed = lax.dot_general(
                    weights, by_head(2, c + k, g), (((0,), (0,)), ((), ())), preferred_element_type=F32
                )
                for t in range(2):
                    scratch[g * 2 + t, pl.ds(c + k, 64, stride=8), :] = mixed[
                        k * 64 : (k + 1) * 64, t * 128 : (t + 1) * 128
                    ]
    mixed = jnp.concatenate([scratch[t].astype(BF) for t in range(6)], axis=1)
    stream[...] += mm(mixed, exit_col[...])

    normed = normalize(stream[...], gain_ffn_ref[...][None, :])
    copies[0].wait()
    for r in range(4):
        rows = slice(r * 128, (r + 1) * 128)
        pre = mm(normed[rows, :], expand[...])
        hidden = (0.5 * pre * (1.0 + lax.erf(pre * math.sqrt(0.5)))).astype(BF)
        if r == 0:
            copies[1].wait()
        done = (stream[rows, :] + mm(hidden, shrink[...])).astype(BF)
        for i, (c, xl) in enumerate((c, xl) for c in range(2) for xl in range(2)):
            out_ref[(xl * 4 + r) * 2 + c] = done[i * 32 : (i + 1) * 32, :]


def column_part(mix, x, gain_col, gain_ffn, exit_row, attend, exit_col, expand, shrink):
    vmem = pl.BlockSpec(memory_space=pltpu.VMEM)
    return pl.pallas_call(
        column_kernel,
        in_specs=[vmem] * 7 + [pl.BlockSpec(memory_space=pltpu.HBM)] * 2,
        out_specs=vmem,
        out_shape=jax.ShapeDtypeStruct((16, 32, 768), BF),
        scratch_shapes=[
            pltpu.VMEM((512, 2304), BF),
            pltpu.VMEM((512, 768), F32),
            pltpu.VMEM((6, 512, 128), F32),
            pltpu.VMEM(expand.shape, BF),
            pltpu.VMEM(shrink.shape, BF),
            pltpu.SemaphoreType.DMA((2,)),
        ],
        compiler_params=params(44),
        name="column_part",
    )(mix, x, gain_col, gain_ffn, exit_row, exit_col, attend, expand, shrink)


def local(
    embeddings,
    gain_row,
    attend_row,
    exit_row,
    gain_col,
    attend_col,
    exit_col,
    gain_ffn,
    expand,
    shrink,
):
    seq, col = lax.axis_index("seq"), lax.axis_index("col")
    core, y, z = seq % 2, seq // 2 % 4, col // 2
    place = jnp.stack([core, col % 2 * 2 + seq // 8, y, z]).astype(jnp.int32)
    scale = E ** (-0.5) / math.sqrt(embeddings.shape[0] * lax.axis_size("seq"))

    normed, *keys = key_proj(place, embeddings.reshape(512, 768), gain_row, attend_row)
    keys = over_x(keys)
    queries_values = query_value_proj(normed, attend_row)
    x = embeddings.reshape(4, 2, 8, 8, 768).transpose(2, 1, 0, 3, 4).reshape(16, 32, 768)
    own, *keys = keys
    keys, own, queries_values = lax.optimization_barrier((jnp.stack(keys), own, queries_values))

    keys_all = gather(keys, Z_COLUMNS)
    own = [own] + [send(own, dz=dz) for dz in (1, 3, 2)]
    queries_values, x = lax.optimization_barrier((swap(queries_values, X_RINGS), x, *own))[:2]
    own = own + [to_other_core(k) for k in own]
    x = lax.all_to_all(x, "seq", split_axis=0, concat_axis=0, tiled=True)
    queries, values = queries_values[:, 0], queries_values[:, 1]
    values = lax.optimization_barrier((values, keys))[0]
    values = gather(values, Z_COLUMNS)

    queries0 = lax.dynamic_slice_in_dim(queries, core * 64, 64, axis=3)
    queries1 = to_other_core(lax.dynamic_slice_in_dim(queries, (1 - core) * 64, 64, axis=3))
    keys = lax.optimization_barrier((keys_all, x, queries1, *own))[0]
    scores = partial_scores(place, queries0, queries1, own, keys)
    scores, x = lax.optimization_barrier((scores, x))
    weights = row_softmax(swap(scores, Y_RINGS), scale)
    values = lax.optimization_barrier((values, weights))[0]
    weights = [weights] + [send(weights, dy=dy) for dy in (3, 2, 1)]
    mix = row_mix(place, weights, values)
    mix = swap(mix, PLANES).reshape(16, 3, 64, 128)

    out = column_part(mix, x, gain_col, gain_ffn, exit_row, attend_col, exit_col, expand, shrink)
    out = lax.all_to_all(out, "seq", split_axis=0, concat_axis=0, tiled=True)
    return out.reshape(8, 2, 4, 8, 768).transpose(2, 1, 0, 3, 4).reshape(4, 128, 768)


def solution(mesh):
    in_specs = (P("seq", "col", None), P(), P(), P(), P(), P(), P(), P(), P(), P())
    out_specs = P("seq", "col", None)
    return jax.shard_map(local, mesh=mesh, in_specs=in_specs, out_specs=out_specs, check_vma=False)
```
